32 devices in a mesh: grp: 4 (over x, core), seq: 8 (over z, y).
Axes of the slice: x: 2, y: 2, z: 4, core: 2. Of those that a mesh axis runs over, the one named last changes fastest.
Arguments:
- tokens: bfloat16 [768, 40960], P('grp', 'seq'), may hold values from -6 to 6
- lengths: int32 [80], P('seq'), may hold values from 32 to 512, as said below
- w_qkv: bfloat16 [768, 576], P('grp'), may hold values from -0.4375 to 0.4375
- b_qv: bfloat16 [2, 768], P(None, 'grp'), may hold values from -2 to 2
- w_out: bfloat16 [768, 768], P('grp'), may hold values from -1.75 to 1.75
- b_out: bfloat16 [768], P('grp'), may hold values from -2 to 2
- ln1_gain: bfloat16 [768], P('grp'), may hold values from 0.25 to 1.75
- ln1_bias: bfloat16 [768], P('grp'), may hold values from -2 to 2
- w_up: bfloat16 [768, 768], P('grp'), may hold values from -0.4375 to 0.4375
- b_up: bfloat16 [3072], P('grp'), may hold values from -2 to 2
- w_down: bfloat16 [768, 768], P('grp'), may hold values from -0.21875 to 0.21875
- b_down: bfloat16 [768], P('grp'), may hold values from -2 to 2
- ln2_gain: bfloat16 [768], P('grp'), may hold values from 0.25 to 1.75
- ln2_bias: bfloat16 [768], P('grp'), may hold values from -2 to 2
- cotangent: bfloat16 [768, 40960], P('grp', 'seq'), may hold values from -6 to 6
Outputs:
- output: bfloat16 [768, 40960], P('grp', 'seq')
- grad_tokens: bfloat16 [768, 40960], P('grp', 'seq')
- grad_w_qkv: float32 [768, 576], P('grp')
- grad_b_qv: float32 [2, 768], P(None, 'grp')
- grad_w_out: float32 [768, 768], P('grp')
- grad_b_out: float32 [768], P('grp')
- grad_ln1_gain: float32 [768], P('grp')
- grad_ln1_bias: float32 [768], P('grp')
- grad_w_up: float32 [768, 768], P('grp')
- grad_b_up: float32 [3072], P('grp')
- grad_w_down: float32 [768, 768], P('grp')
- grad_b_down: float32 [768], P('grp')
- grad_ln2_gain: float32 [768], P('grp')
- grad_ln2_bias: float32 [768], P('grp')
The draws below stay inside these ranges and needn't reach their ends.
Inputs may be any that keep to these rules, and one draw needn't show every extreme that they name: `lengths`: live positions of each slot of 512; some sequence has exactly 512 and some exactly 32.
All inputs are finite; a program needn't handle non-finite values.
Results may differ from the reference program's by a relative error of at most 0.014.
Values may be sent and summed in bfloat16 or wider, within the bound.
No kernel may reach another device: no remote copies, remote signals or barrier semaphores. Data moves between devices by JAX's collectives and lax.ppermute only.
A program may use at most 128 MiB of HBM per device.

```python
import math
import jax
import jax.numpy as jnp
from jax import lax

D = 768
HEADS = 12
HDIM = 64
FF = 3072
GROUPS = 4
SLOT = 512
SHORTEST = 32
SEQ_DEV = 10
SEQS = 80
TOKENS = 40960


def draw_lengths(key, part):
    key = jax.random.fold_in(key, 7)
    first_key, second_key = jax.random.split(key)
    lengths_drawn = jax.random.randint(first_key, (SEQS,), SHORTEST, SLOT + 1, dtype=jnp.int32)
    shuffled = jax.random.permutation(second_key, SEQS)
    lengths_drawn = lengths_drawn.at[shuffled[0]].set(SLOT)
    lengths_drawn = lengths_drawn.at[shuffled[1]].set(SHORTEST)
    return lengths_drawn


def block_scale(stream_key, extent, cuts, least, largest):
    def one(dim, blocks):
        draws = jax.random.uniform(jax.random.fold_in(jax.random.fold_in(stream_key, 6), dim), (blocks,), jnp.float32, least / len(cuts), largest / len(cuts))
        return jnp.repeat(jnp.exp(draws), extent[dim] // blocks).reshape((-1,) + (1,) * (len(extent) - dim - 1))

    level = one(*cuts[0])
    for cut in cuts[1:]:
        level = level * one(*cut)
    return level


def centred(rng, dims, deviation, bound, cuts=(), kind=jnp.bfloat16):
    level = block_scale(rng, dims, cuts, -0.22, 0.18) if cuts else 1.0
    values = jax.random.normal(rng, dims, jnp.float32) * deviation * level
    return jnp.minimum(jnp.maximum(values, -bound), bound).astype(kind)


def setup_inputs(seed: int = 0) -> dict:
    streams_of = jax.random.split(jax.random.key(seed), 16)
    tokens = centred(streams_of[0], (D, TOKENS), 1.0, 6.0, ((0, 4), (1, 8)))
    lengths = draw_lengths(jax.random.fold_in(streams_of[15], 71), 0)
    w_qkv = centred(streams_of[2], (D, 3 * D // GROUPS), (D // GROUPS) ** -0.5, 0.4375, ((0, 4),))
    b_qv = centred(streams_of[3], (2, D), 0.3, 2.0, ((1, 4),))
    w_out = centred(streams_of[4], (D, D), (max(D // 64, 1)) ** -0.5, 1.75, ((0, 4),))
    b_out = centred(streams_of[5], (D,), 0.3, 2.0, ((0, 4),))
    ln1_gain = jnp.clip(1.0 + 0.15 * jax.random.normal(streams_of[6], (D,), jnp.float32), 0.25, 1.75).astype(jnp.bfloat16)
    ln1_bias = centred(streams_of[7], (D,), 0.3, 2.0, ((0, 4),))
    w_up = centred(streams_of[8], (D, FF // GROUPS), (D // GROUPS) ** -0.5, 0.4375, ((0, 4),))
    b_up = centred(streams_of[9], (FF,), 0.3, 2.0, ((0, 4),))
    w_down = centred(streams_of[10], (D, FF // GROUPS), (FF // GROUPS) ** -0.5, 0.21875, ((0, 4),))
    b_down = centred(streams_of[11], (D,), 0.3, 2.0, ((0, 4),))
    ln2_gain = jnp.clip(1.0 + 0.15 * jax.random.normal(streams_of[12], (D,), jnp.float32), 0.25, 1.75).astype(jnp.bfloat16)
    ln2_bias = centred(streams_of[13], (D,), 0.3, 2.0, ((0, 4),))
    cotangent = centred(streams_of[14], (D, TOKENS), 1.0, 6.0, ((0, 4), (1, 8)))
    return {"tokens": tokens, "lengths": lengths, "w_qkv": w_qkv, "b_qv": b_qv, "w_out": w_out, "b_out": b_out, "ln1_gain": ln1_gain, "ln1_bias": ln1_bias, "w_up": w_up, "b_up": b_up, "w_down": w_down, "b_down": b_down, "ln2_gain": ln2_gain, "ln2_bias": ln2_bias, "cotangent": cotangent}


@jax.custom_vjp
def low(v):
    return lax.optimization_barrier(v.astype(jnp.bfloat16)).astype(jnp.float32)

@jax.custom_vjp
def low_back(v):
    return v

def low_keep(v):
    return (low(v), None)

def low_pass(kept, grad):
    return (grad,)

def back_keep(v):
    return (v, None)

def back_low(kept, grad):
    return (low(grad),)
low.defvjp(low_keep, low_pass)
low_back.defvjp(back_keep, back_low)
PRECISE = lax.Precision.HIGHEST
EPSILON = 1e-06
MASKED_SCORE = -1000000000.0

def matmul(left, right):
    return jnp.dot(left, right, precision=PRECISE, preferred_element_type=jnp.float32)

def grouped(inputs, weight):
    row_count = inputs.shape[0]
    split_in = inputs.reshape(row_count, GROUPS, inputs.shape[1] // GROUPS)
    split_weight = weight.reshape(GROUPS, weight.shape[0] // GROUPS, weight.shape[1])
    return jnp.einsum('rgc,gcn->rgn', split_in, split_weight, precision=PRECISE)

def normalize(resid, gain, shift):
    center = lax.optimization_barrier(jnp.mean(resid, axis=-1, keepdims=True))
    spread = lax.optimization_barrier(jnp.mean((resid - center) * (resid - center), axis=-1, keepdims=True))
    return (resid - center) * lax.rsqrt(spread + EPSILON) * gain + shift

def gelu(pre_act):
    return 0.5 * pre_act * (1.0 + lax.erf(pre_act * 0.7071067811865476))

def attend(block_item):
    query_rows, key_rows, value_rows, live_keys = block_item
    query_heads = query_rows.reshape(SLOT, HEADS, HDIM)
    key_heads = key_rows.reshape(SLOT, HEADS, HDIM)
    value_heads = value_rows.reshape(SLOT, HEADS, HDIM)
    scores = low_back(jnp.einsum('qhd,khd->hqk', query_heads, key_heads, precision=PRECISE) * (1.0 / math.sqrt(HDIM)))
    scores = jnp.where(live_keys[None, None, :] > 0.5, scores, MASKED_SCORE)
    highest = lax.optimization_barrier(jnp.max(scores, axis=-1, keepdims=True))
    weights = jnp.exp(scores - highest)
    probs = low(weights / lax.optimization_barrier(jnp.sum(weights, axis=-1, keepdims=True)))
    return jnp.einsum('hqk,khd->qhd', probs, value_heads, precision=PRECISE).reshape(SLOT, D)

def layer(tokens_in, w_qkv, b_qv, w_out, b_out, ln1_gain, ln1_bias, w_up, b_up, w_down, b_down, ln2_gain, ln2_bias, live):
    row_count = tokens_in.shape[0]
    seq_count = row_count // SLOT
    width = D // GROUPS
    down_by_input = w_down.reshape(GROUPS, width, FF // GROUPS).transpose(0, 2, 1).reshape(FF, width)
    projected = grouped(tokens_in, w_qkv)
    queries = low_back(low(projected[:, :, :width].reshape(row_count, D) + b_qv[0]))
    key_rows = low_back(low(projected[:, :, width:2 * width].reshape(row_count, D)))
    value_rows = low_back(low(projected[:, :, 2 * width:].reshape(row_count, D) + b_qv[1]))
    context = lax.map(jax.checkpoint(attend), (queries.reshape(seq_count, SLOT, D), key_rows.reshape(seq_count, SLOT, D), value_rows.reshape(seq_count, SLOT, D), live.reshape(seq_count, SLOT)))
    context = low_back(low(context.reshape(row_count, D)))
    resid_one = low_back(tokens_in + matmul(context, w_out) + b_out)
    hidden = low_back(low(normalize(resid_one, ln1_gain, ln1_bias)))
    pre_act = low_back(grouped(hidden, w_up).reshape(row_count, FF) + b_up)
    act = low(gelu(pre_act))
    resid_two = low_back(hidden + grouped(act, down_by_input).reshape(row_count, D) + b_down)
    return normalize(resid_two, ln2_gain, ln2_bias) * live[:, None]

def reference(tokens, lengths, w_qkv, b_qv, w_out, b_out, ln1_gain, ln1_bias, w_up, b_up, w_down, b_down, ln2_gain, ln2_bias, cotangent):
    params = (w_qkv.astype(jnp.float32), b_qv.astype(jnp.float32), w_out.astype(jnp.float32), b_out.astype(jnp.float32), ln1_gain.astype(jnp.float32), ln1_bias.astype(jnp.float32), w_up.astype(jnp.float32), b_up.astype(jnp.float32), w_down.astype(jnp.float32), b_down.astype(jnp.float32), ln2_gain.astype(jnp.float32), ln2_bias.astype(jnp.float32))
    block_rows = SEQ_DEV * SLOT
    block_count = TOKENS // block_rows
    positions = jnp.arange(SLOT, dtype=jnp.int32)
    live_rows = (positions[None, :] < lengths[:, None]).astype(jnp.float32).reshape(block_count, block_rows)
    inputs = tokens.astype(jnp.float32).T.reshape(block_count, block_rows, D)
    upstream = cotangent.astype(jnp.float32).T.reshape(block_count, block_rows, D)

    def step(carry, block_item):
        tokens_blk, live_blk, upstream_blk = block_item

        def forward(tokens_in, *weights):
            return layer(tokens_in, *weights, live_blk)
        result, pull = jax.vjp(forward, tokens_blk, *params)
        grads = pull(upstream_blk)
        summed = tuple((earlier + latest for earlier, latest in zip(carry, grads[1:])))
        return (summed, (result.astype(jnp.bfloat16), grads[0].astype(jnp.bfloat16)))
    zeros = tuple((jnp.zeros_like(weight) for weight in params))
    totals, (results, grad_rows) = lax.scan(step, zeros, (inputs, live_rows, upstream))
    return (results.reshape(TOKENS, D).T, grad_rows.reshape(TOKENS, D).T, totals[0], totals[1], totals[2], totals[3], totals[4], totals[5], totals[6], totals[7], totals[8], totals[9], totals[10], totals[11])
```

```python
import functools
import math

import jax
import jax.numpy as jnp
from jax import lax
from jax.experimental import pallas as pl
from jax.experimental.pallas import tpu as pltpu
from jax.sharding import PartitionSpec as P

D = 768
HDIM = 64
SLOT = 512
LANE = 128
GROUPS = 4
EPSILON = 1e-06
MASKED_SCORE = -1000000000.0
SCALE = 1.0 / math.sqrt(HDIM)
CHUNKS = 2
F32 = jnp.float32
BF16 = jnp.bfloat16


def nn(left, right):
    return lax.dot_general(left, right, (((1,), (0,)), ((), ())), preferred_element_type=F32)


def tn(left, right):
    return lax.dot_general(left, right, (((0,), (0,)), ((), ())), preferred_element_type=F32)


def nt(left, right):
    return lax.dot_general(left, right, (((1,), (1,)), ((), ())), preferred_element_type=F32)


def for_length(length, body):
    blocks = (length + (LANE - 1)) // LANE
    for count in range(1, SLOT // LANE + 1):
        pl.when(blocks == count)(functools.partial(body, count * LANE))


def fold(array):
    total = array[:, :LANE]
    for start in range(LANE, array.shape[1], LANE):
        total = total + array[:, start : start + LANE]
    return total


def live_row(length, columns):
    return (lax.broadcasted_iota(jnp.int32, (1, columns), 1) < length).astype(F32)


def mask_keys(scores, length):
    columns = scores.shape[0]
    start = columns - LANE
    last = scores[start:]
    key = lax.broadcasted_iota(jnp.int32, last.shape, 0) + start
    last = jnp.where(key < length, last, MASKED_SCORE)
    return last if start == 0 else jnp.concatenate([scores[:start], last], axis=0)


def gelu_pair(pre_act):
    normal_cdf = 0.5 * (1.0 + lax.erf(pre_act * 0.7071067811865476))
    density = jnp.exp(-0.5 * pre_act * pre_act) * 0.3989422804014327
    return pre_act * normal_cdf, normal_cdf + pre_act * density


def colsum(array):
    return jnp.sum(array, axis=0, keepdims=True)


def attend_forward_kernel(first, lens, tok, wqkv_t, vec, ctx, qkv, lse):
    length = lens[first + pl.program_id(0)]
    width = tok.shape[0]

    def body(columns):
        cols = slice(0, columns)
        proj = nn(wqkv_t[...], tok[:, cols])
        query = ((proj[:width] + vec[:, 0:1]) * SCALE).astype(BF16)
        key = proj[width : 2 * width].astype(BF16)
        value = (proj[2 * width :] + vec[:, 1:2]).astype(BF16)
        qkv[:width, cols] = query
        qkv[width : 2 * width, cols] = key
        qkv[2 * width :, cols] = value
        for head in range(width // HDIM):
            rows = slice(head * HDIM, (head + 1) * HDIM)
            scores = mask_keys(tn(key[rows], query[rows]), length)
            highest = jnp.max(scores, axis=0, keepdims=True)
            weights = jnp.exp(scores - highest)
            total = colsum(weights)
            ctx[rows, cols] = (nn(value[rows], weights.astype(BF16)) * (1.0 / total)).astype(BF16)
            lse[head : head + 1, cols] = highest + jnp.log(total)
        if columns < SLOT:
            ctx[:, columns:] = jnp.zeros((width, SLOT - columns), BF16)

    for_length(length, body)


def mix_kernel(first, lens, ctx0, ctx1, ctx2, ctx3, tok, wo_t, vec, resid, stats):
    length = lens[first + pl.program_id(0)]

    def body(columns):
        cols = slice(0, columns)
        total = tok[:, cols].astype(F32) + vec[:, 2:3]
        for place, ctx in enumerate((ctx0, ctx1, ctx2, ctx3)):
            total = total + nn(wo_t[place], ctx[:, cols])
        resid[:, cols] = total
        stats[0:1, cols] = colsum(total)
        stats[1:2, cols] = colsum(total * total)

    for_length(length, body)


def first_norm(stats, cols):
    total = stats[0][:, cols] + stats[1][:, cols] + stats[2][:, cols] + stats[3][:, cols]
    mean = total[0:1] / D
    inverse = lax.rsqrt(total[1:2] / D - mean * mean + EPSILON)
    return mean, inverse


def feed_forward_kernel(
    first, lens, resid, sa, sb, sc, sd, cot, wup_t, wdown, vec, bup, hid, act, slope, two, stats
):
    length = lens[first + pl.program_id(0)]

    def body(columns):
        cols = slice(0, columns)
        mean, inverse = first_norm((sa, sb, sc, sd), cols)
        normed = (resid[:, cols] - mean) * inverse
        hidden = (normed * vec[:, 3:4] + vec[:, 4:5]).astype(BF16)
        hid[:, cols] = hidden
        pre_act = nn(wup_t[...], hidden) + bup[:, 0:1]
        activated, gradient = gelu_pair(pre_act)
        activated = activated.astype(BF16)
        act[:, cols] = activated
        slope[:, cols] = gradient.astype(BF16)
        resid_two = hidden.astype(F32) + nn(wdown[...], activated) + vec[:, 5:6]
        two[:, cols] = resid_two
        grad = cot[:, cols].astype(F32) * live_row(length, columns) * vec[:, 6:7]
        stats[0:1, cols] = colsum(resid_two)
        stats[1:2, cols] = colsum(resid_two * resid_two)
        stats[2:3, cols] = colsum(grad)
        stats[3:4, cols] = colsum(grad * resid_two)

    for_length(length, body)


def feed_backward_kernel(
    first, lens, two, ta, tb, tc, td, cot, slope, resid, sa, sb, sc, sd, wdown_t, wup, vec,
    out, gtwo, gpre, ghid, stats, sums, sums_up,
):
    length = lens[first + pl.program_id(0)]

    @pl.when(pl.program_id(0) == 0)
    def _():
        sums[...] = jnp.zeros_like(sums)
        sums_up[...] = jnp.zeros_like(sums_up)

    def body(columns):
        cols = slice(0, columns)
        total = ta[:, cols] + tb[:, cols] + tc[:, cols] + td[:, cols]
        mean_two = total[0:1] / D
        inverse_two = lax.rsqrt(total[1:2] / D - mean_two * mean_two + EPSILON)
        normed_two = (two[:, cols] - mean_two) * inverse_two
        live = live_row(length, columns)
        out[:, cols] = ((normed_two * vec[:, 6:7] + vec[:, 7:8]) * live).astype(BF16)
        if columns < SLOT:
            out[:, columns:] = jnp.zeros((out.shape[0], SLOT - columns), BF16)
        upstream = cot[:, cols].astype(F32) * live
        sums[0] += fold(upstream * normed_two)
        sums[1] += fold(upstream)
        plain = total[2:3] / D
        weighted = inverse_two * (total[3:4] - mean_two * total[2:3]) / D
        grad_two = (
            inverse_two * (upstream * vec[:, 6:7] - plain - normed_two * weighted)
        ).astype(BF16)
        gtwo[:, cols] = grad_two
        grad_two_wide = grad_two.astype(F32)
        sums[2] += fold(grad_two_wide)
        grad_pre = (nn(wdown_t[...], grad_two) * slope[:, cols].astype(F32)).astype(BF16)
        gpre[:, cols] = grad_pre
        sums_up[...] += fold(grad_pre.astype(F32))
        grad_hidden = (grad_two_wide + nn(wup[...], grad_pre)).astype(BF16)
        ghid[:, cols] = grad_hidden
        grad_hidden = grad_hidden.astype(F32)
        mean, inverse = first_norm((sa, sb, sc, sd), cols)
        normed = (resid[:, cols] - mean) * inverse
        sums[3] += fold(grad_hidden * normed)
        sums[4] += fold(grad_hidden)
        grad = grad_hidden * vec[:, 3:4]
        stats[0:1, cols] = colsum(grad)
        stats[1:2, cols] = colsum(grad * normed)

    for_length(length, body)


def residual_grad_kernel(
    first, lens, ghid, ua, ub, uc, ud, resid, sa, sb, sc, sd, vec, gone, sums
):
    length = lens[first + pl.program_id(0)]

    @pl.when(pl.program_id(0) == 0)
    def _():
        sums[...] = jnp.zeros_like(sums)

    def body(columns):
        cols = slice(0, columns)
        mean, inverse = first_norm((sa, sb, sc, sd), cols)
        normed = (resid[:, cols] - mean) * inverse
        total = (ua[:, cols] + ub[:, cols] + uc[:, cols] + ud[:, cols]) / D
        grad = ghid[:, cols].astype(F32) * vec[:, 3:4]
        grad_one = (inverse * (grad - total[0:1] - normed * total[1:2])).astype(BF16)
        gone[:, cols] = grad_one
        sums[...] += fold(grad_one.astype(F32))

    for_length(length, body)


def weight_grad_kernel(
    first, lens, gtwo, act, hid, gpre, gone, ctx0, ctx1, ctx2, ctx3, dwdown, dwup, dwo
):
    length = lens[first + pl.program_id(0)]

    @pl.when(pl.program_id(0) == 0)
    def _():
        dwdown[...] = jnp.zeros_like(dwdown)
        dwup[...] = jnp.zeros_like(dwup)
        dwo[...] = jnp.zeros_like(dwo)

    def body(columns):
        cols = slice(0, columns)
        dwdown[...] += nt(gtwo[:, cols], act[:, cols])
        dwup[...] += nt(hid[:, cols], gpre[:, cols])
        for place, ctx in enumerate((ctx0, ctx1, ctx2, ctx3)):
            dwo[place] += nt(ctx[:, cols], gone[:, cols])

    for_length(length, body)


def attend_backward_kernel(
    first, lens, g0, g1, g2, g3, qkv, lse, tok, wo, wqkv, gtok, dwqkv, sums, gqkv
):
    length = lens[first + pl.program_id(0)]
    width = tok.shape[0]

    @pl.when(pl.program_id(0) == 0)
    def _():
        dwqkv[...] = jnp.zeros_like(dwqkv)
        sums[...] = jnp.zeros_like(sums)

    def body(columns):
        cols = slice(0, columns)
        grad_context = nn(wo[0], g0[:, cols])
        for place, grad in ((1, g1), (2, g2), (3, g3)):
            grad_context = grad_context + nn(wo[place], grad[:, cols])
        grad_context = grad_context.astype(BF16)
        for head in range(width // HDIM):
            start = head * HDIM
            rows = slice(start, start + HDIM)
            query = qkv[rows, cols]
            key = qkv[width + start : width + start + HDIM, cols]
            value = qkv[2 * width + start : 2 * width + start + HDIM, cols]
            grad = grad_context[rows]
            scores = mask_keys(tn(key, query), length)
            probs = jnp.exp(scores - lse[head : head + 1, cols])
            grad_probs = tn(value, grad)
            inner = colsum(grad_probs * probs)
            grad_scores = (probs * (grad_probs - inner)).astype(BF16)
            gqkv[rows, cols] = (nn(key, grad_scores) * SCALE).astype(BF16)
            gqkv[width + start : width + start + HDIM, cols] = nt(query, grad_scores).astype(BF16)
            gqkv[2 * width + start : 2 * width + start + HDIM, cols] = nt(
                grad, probs.astype(BF16)
            ).astype(BF16)
        grad_proj = gqkv[:, cols]
        sums[0] += fold(grad_proj[:width].astype(F32))
        sums[1] += fold(grad_proj[2 * width :].astype(F32))
        dwqkv[...] += nt(tok[:, cols], grad_proj)
        gtok[:, cols] = (nn(wqkv[...], grad_proj) + g0[:, cols].astype(F32)).astype(BF16)
        if columns < SLOT:
            gtok[:, columns:] = jnp.zeros((width, SLOT - columns), BF16)

    for_length(length, body)


def slots(rows, offset=0):
    return pl.BlockSpec((rows, SLOT), lambda i, lens: (0, i + offset))


def whole(*shape):
    return pl.BlockSpec(shape, lambda i, lens: (0,) * len(shape))


def call(kernel, name, first, count, lengths, ins, outs, scratch=()):
    return pl.pallas_call(
        functools.partial(kernel, first),
        out_shape=[jax.ShapeDtypeStruct(shape, kind) for shape, kind, _ in outs],
        grid_spec=pltpu.PrefetchScalarGridSpec(
            num_scalar_prefetch=1,
            grid=(count,),
            in_specs=[block for _, block in ins],
            out_specs=[block for _, _, block in outs],
            scratch_shapes=list(scratch),
        ),
        compiler_params=pltpu.CompilerParams(
            dimension_semantics=("arbitrary",), vmem_limit_bytes=48 * 2**20
        ),
        cost_estimate=pl.CostEstimate(flops=0, bytes_accessed=0, transcendentals=0),
        name=name,
    )(lengths, *[array for array, _ in ins])


def permute(array, flip):
    return lax.ppermute(array, "grp", [(g, g ^ flip) for g in range(GROUPS)])


def gather_wide(array):
    across = permute(array, 2)
    return [array, permute(array, 1), across, permute(across, 1)]


def gather_small(array):
    return [array] + [permute(array, flip) for flip in (1, 2, 3)]


def sum_over_seq(pieces):
    ranks = lax.axis_size("seq")
    packed = jnp.concatenate([piece.astype(BF16) for piece in pieces], axis=1)
    rows, columns = packed.shape
    shares = lax.all_to_all(packed.reshape(ranks, rows // ranks, columns), "seq", 0, 0)
    own = jnp.sum(shares.astype(F32), axis=0).astype(BF16)
    spread = lax.all_to_all(jnp.broadcast_to(own[None], shares.shape), "seq", 0, 0)
    total = spread.reshape(rows, columns).astype(F32)
    result, start = [], 0
    for piece in pieces:
        result.append(total[:, start : start + piece.shape[1]])
        start += piece.shape[1]
    return result


def local(
    tokens, lengths, w_qkv, b_qv, w_out, b_out, ln1_gain, ln1_bias, w_up, b_up, w_down, b_down,
    ln2_gain, ln2_bias, cotangent,
):
    width = tokens.shape[0]
    hidden_width = w_up.shape[1]
    seq_count = lengths.shape[0]
    group = lax.axis_index("grp")
    vec = jnp.stack(
        [b_qv[0], b_qv[1], b_out, ln1_gain, ln1_bias, b_down, ln2_gain, ln2_bias], axis=1
    ).astype(F32)
    bup = b_up.astype(F32)[:, None]
    wqkv_t = w_qkv.T
    blocks_in = w_out.reshape(width, GROUPS, width).transpose(1, 0, 2)
    wo = jnp.stack([lax.dynamic_index_in_dim(blocks_in, group ^ r, 0, False) for r in range(GROUPS)])
    wo_t = jnp.stack(
        [wo[0].T] + [permute(wo[flip].T, flip) for flip in (1, 2, 3)]
    )
    wup_t, wdown_t = w_up.T, w_down.T
    bounds = [seq_count * part // CHUNKS for part in range(CHUNKS + 1)]
    chunks = [(a, b - a) for a, b in zip(bounds[:-1], bounds[1:])]
    vec_in, bup_in = (vec, whole(width, 8)), (bup, whole(hidden_width, 1))

    forward = []
    for first, count in chunks:
        rows = count * SLOT
        forward.append(
            call(
                attend_forward_kernel, "attend_forward", first, count, lengths,
                [(tokens, slots(width, first)), (wqkv_t, whole(3 * width, width)), vec_in],
                [
                    ((width, rows), BF16, slots(width)),
                    ((3 * width, rows), BF16, slots(3 * width)),
                    ((8, rows), F32, slots(8)),
                ],
            )
        )
    contexts = [gather_wide(ctx) for ctx, _, _ in forward]
    mids = []
    for (first, count), ctx in zip(chunks, contexts):
        rows = count * SLOT
        resid, stats_one = call(
            mix_kernel, "mix", first, count, lengths,
            [(c, slots(width)) for c in ctx]
            + [(tokens, slots(width, first)), (wo_t, whole(GROUPS, width, width)), vec_in],
            [((width, rows), F32, slots(width)), ((2, rows), F32, slots(2))],
        )
        one = [(s, slots(2)) for s in gather_small(stats_one)]
        hid, act, slope, two, stats_two = call(
            feed_forward_kernel, "feed_forward", first, count, lengths,
            [(resid, slots(width))] + one + [
                (cotangent, slots(width, first)), (wup_t, whole(hidden_width, width)),
                (w_down, whole(width, hidden_width)), vec_in, bup_in,
            ],
            [
                ((width, rows), BF16, slots(width)),
                ((hidden_width, rows), BF16, slots(hidden_width)),
                ((hidden_width, rows), BF16, slots(hidden_width)),
                ((width, rows), F32, slots(width)),
                ((4, rows), F32, slots(4)),
            ],
        )
        out, gtwo, gpre, ghid, stats_three, sums, sums_up = call(
            feed_backward_kernel, "feed_backward", first, count, lengths,
            [(two, slots(width))] + [(s, slots(4)) for s in gather_small(stats_two)] + [
                (cotangent, slots(width, first)), (slope, slots(hidden_width)),
                (resid, slots(width)),
            ] + one + [
                (wdown_t, whole(hidden_width, width)), (w_up, whole(width, hidden_width)), vec_in,
            ],
            [
                ((width, rows), BF16, slots(width)),
                ((width, rows), BF16, slots(width)),
                ((hidden_width, rows), BF16, slots(hidden_width)),
                ((width, rows), BF16, slots(width)),
                ((2, rows), F32, slots(2)),
                ((5, width, LANE), F32, whole(5, width, LANE)),
                ((hidden_width, LANE), F32, whole(hidden_width, LANE)),
            ],
        )
        gone, sums_out = call(
            residual_grad_kernel, "residual_grad", first, count, lengths,
            [(ghid, slots(width))] + [(s, slots(2)) for s in gather_small(stats_three)]
            + [(resid, slots(width))] + one + [vec_in],
            [((width, rows), BF16, slots(width)), ((width, LANE), F32, whole(width, LANE))],
        )
        mids.append((hid, act, gtwo, gpre, gone, out, sums, sums_up, sums_out))
    gones = [gather_wide(mid[4]) for mid in mids]
    weights = []
    for (first, count), ctx, mid in zip(chunks, contexts, mids):
        hid, act, gtwo, gpre, gone = mid[:5]
        weights.append(
            call(
                weight_grad_kernel, "weight_grad", first, count, lengths,
                [
                    (gtwo, slots(width)), (act, slots(hidden_width)), (hid, slots(width)),
                    (gpre, slots(hidden_width)), (gone, slots(width)),
                ] + [(c, slots(width)) for c in ctx],
                [
                    ((width, hidden_width), F32, whole(width, hidden_width)),
                    ((width, hidden_width), F32, whole(width, hidden_width)),
                    ((GROUPS, width, width), F32, whole(GROUPS, width, width)),
                ],
            )
        )
    backward = []
    for (first, count), gone, (_, qkv, lse) in zip(chunks, gones, forward):
        rows = count * SLOT
        backward.append(
            call(
                attend_backward_kernel, "attend_backward", first, count, lengths,
                [(g, slots(width)) for g in gone] + [
                    (qkv, slots(3 * width)), (lse, slots(8)), (tokens, slots(width, first)),
                    (wo, whole(GROUPS, width, width)), (w_qkv, whole(width, 3 * width)),
                ],
                [
                    ((width, rows), BF16, slots(width)),
                    ((width, 3 * width), F32, whole(width, 3 * width)),
                    ((2, width, LANE), F32, whole(2, width, LANE)),
                ],
                scratch=[pltpu.VMEM((3 * width, SLOT), BF16)],
            )
        )

    def added(parts):
        total = parts[0]
        for part in parts[1:]:
            total = total + part
        return total

    dwdown, dwup, dwo = (added([w[i] for w in weights]) for i in range(3))
    small = jnp.sum(added([mid[6] for mid in mids]), axis=2).T
    small_out = jnp.sum(added([mid[8] for mid in mids]), axis=1)[:, None]
    small_up = jnp.sum(added([mid[7] for mid in mids]), axis=1).reshape(GROUPS, width).T
    dwo = dwo.astype(BF16)
    routed = [dwo[0]] + [permute(dwo[flip], flip) for flip in (1, 2, 3)]
    dwdown, dwup, *dwo, small, small_out, small_up = sum_over_seq(
        [dwdown, dwup] + routed + [small, small_out, small_up]
    )
    dwqkv = added([b[1] for b in backward])
    small_qv = jnp.sum(added([b[2] for b in backward]), axis=2).T
    dwqkv, small_qv = sum_over_seq([dwqkv, small_qv])
    by_place = jnp.stack(dwo)
    grad_w_out = jnp.concatenate(
        [lax.dynamic_index_in_dim(by_place, group ^ t, 0, False) for t in range(GROUPS)], axis=1
    )
    output = jnp.concatenate([mid[5] for mid in mids], axis=1)
    grad_tokens = jnp.concatenate([b[0] for b in backward], axis=1)
    return (
        output, grad_tokens, dwqkv, small_qv.T, grad_w_out, small_out[:, 0], small[:, 3],
        small[:, 4], dwup, small_up.T.reshape(-1), dwdown, small[:, 2], small[:, 0], small[:, 1],
    )


def solution(mesh):
    row, vector = P("grp", None), P("grp")
    placed = (
        P("grp", "seq"), P("seq"), row, P(None, "grp"), row, vector, vector, vector, row, vector,
        row, vector, vector, vector, P("grp", "seq"),
    )
    results = (
        P("grp", "seq"), P("grp", "seq"), row, P(None, "grp"), row, vector, vector, vector, row,
        vector, row, vector, vector, vector,
    )
    return jax.shard_map(local, mesh=mesh, in_specs=placed, out_specs=results, check_vma=False)
```

```python
import functools
import math

import jax
import jax.numpy as jnp
from jax import lax
from jax.experimental import pallas as pl
from jax.experimental.pallas import tpu as pltpu
from jax.sharding import PartitionSpec as P

D = 768
HDIM = 64
SLOT = 512
LANE = 128
GROUPS = 4
EPSILON = 1e-06
MASKED_SCORE = -1000000000.0
SCALE = 1.0 / math.sqrt(HDIM)
CHUNKS = 2
CONTEXT_WAYS = ("permute", "permute")
GRADIENT_WAYS = ("permute", "permute")
COST = 1.0
F32 = jnp.float32
BF16 = jnp.bfloat16


def nn(left, right):
    return lax.dot_general(left, right, (((1,), (0,)), ((), ())), preferred_element_type=F32)


def tn(left, right):
    return lax.dot_general(left, right, (((0,), (0,)), ((), ())), preferred_element_type=F32)


def nt(left, right):
    return lax.dot_general(left, right, (((1,), (1,)), ((), ())), preferred_element_type=F32)


def for_length(length, body):
    blocks = (length + (LANE - 1)) // LANE
    for count in range(1, SLOT // LANE + 1):
        pl.when(blocks == count)(functools.partial(body, count * LANE))


def fold(array):
    total = array[:, :LANE]
    for start in range(LANE, array.shape[1], LANE):
        total = total + array[:, start : start + LANE]
    return total


def live_row(length, columns):
    return (lax.broadcasted_iota(jnp.int32, (1, columns), 1) < length).astype(F32)


def mask_keys(scores, length):
    columns = scores.shape[0]
    start = columns - LANE
    last = scores[start:]
    key = lax.broadcasted_iota(jnp.int32, last.shape, 0) + start
    last = jnp.where(key < length, last, MASKED_SCORE)
    return last if start == 0 else jnp.concatenate([scores[:start], last], axis=0)


def gelu_pair(pre_act):
    normal_cdf = 0.5 * (1.0 + lax.erf(pre_act * 0.7071067811865476))
    density = jnp.exp(-0.5 * pre_act * pre_act) * 0.3989422804014327
    return pre_act * normal_cdf, normal_cdf + pre_act * density


def colsum(array):
    return jnp.sum(array, axis=0, keepdims=True)


def rowsum(array):
    return jnp.sum(array, axis=1, keepdims=True)


def mixers_kernel(lens, group, w_out, wo, wo_t, flat):
    width = w_out.shape[0]
    flat[...] = jnp.transpose(w_out[...])
    for flip in range(GROUPS):
        start = pl.multiple_of((group[0] ^ flip) * width, width)
        block = flat[pl.ds(start, width), :]
        wo_t[flip] = block
        wo[flip] = jnp.transpose(block)


def prepare_kernel(lens, group, rows, w_up, w_down, vec, bup, wup_t, wdown_t):
    width = w_up.shape[0]
    vectors = jnp.transpose(rows[...].astype(F32))
    vec[...] = vectors
    for part in range(bup.shape[0] // width):
        bup[part * width : (part + 1) * width, :] = vectors[:, 8 + part : 9 + part]
    wup_t[...] = jnp.transpose(w_up[...])
    wdown_t[...] = jnp.transpose(w_down[...])


def share_kernel(lens, group, shares, *rest):
    own = rest[-1]
    total = shares[0].astype(F32)
    for place in range(1, shares.shape[0]):
        total = total + shares[place].astype(F32)
    own[...] = jnp.broadcast_to(total.astype(BF16)[None], own.shape)


def attend_forward_kernel(first, lens, group, tok, wqkv, bias, ctx, qkv, lse, wqkv_t, cols_qv):
    length = lens[first + pl.program_id(0)]
    width = tok.shape[0]

    @pl.when(pl.program_id(0) == 0)
    def _():
        wqkv_t[...] = jnp.transpose(wqkv[...])
        cols_qv[...] = jnp.transpose(jnp.concatenate([bias[...].astype(F32)] * 4, axis=0))

    def body(columns):
        cols = slice(0, columns)
        proj = nn(wqkv_t[...], tok[:, cols])
        query = ((proj[:width] + cols_qv[:, 0:1]) * SCALE).astype(BF16)
        key = proj[width : 2 * width].astype(BF16)
        value = (proj[2 * width :] + cols_qv[:, 1:2]).astype(BF16)
        qkv[:width, cols] = query
        qkv[width : 2 * width, cols] = key
        qkv[2 * width :, cols] = value
        for head in range(width // HDIM):
            rows = slice(head * HDIM, (head + 1) * HDIM)
            scores = mask_keys(tn(key[rows], query[rows]), length)
            highest = jnp.max(scores, axis=0, keepdims=True)
            weights = jnp.exp(scores - highest)
            total = colsum(weights)
            ctx[rows, cols] = (nn(value[rows], weights.astype(BF16)) * (1.0 / total)).astype(BF16)
            lse[head : head + 1, cols] = highest + jnp.log(total)
        if columns < SLOT:
            ctx[:, columns:] = jnp.zeros((width, SLOT - columns), BF16)

    for_length(length, body)


def mix_kernel(first, lens, group, ctx0, ctx1, ctx2, ctx3, tok, wo0, wo1, wo2, wo3, vec, resid, stats):
    length = lens[first + pl.program_id(0)]

    def body(columns):
        cols = slice(0, columns)
        total = tok[:, cols].astype(F32) + vec[:, 2:3]
        for weight, ctx in ((wo0, ctx0), (wo1, ctx1), (wo2, ctx2), (wo3, ctx3)):
            total = total + nn(weight[...], ctx[:, cols])
        resid[:, cols] = total
        stats[0:1, cols] = colsum(total)
        stats[1:2, cols] = colsum(total * total)

    for_length(length, body)


def first_norm(stats, cols):
    total = stats[0][:, cols] + stats[1][:, cols] + stats[2][:, cols] + stats[3][:, cols]
    mean = total[0:1] / D
    inverse = lax.rsqrt(total[1:2] / D - mean * mean + EPSILON)
    return mean, inverse


def feed_forward_kernel(
    first, lens, group, resid, sa, sb, sc, sd, cot, wup_t, wdown, vec, bup,
    hid, act, slope, two, stats,
):
    length = lens[first + pl.program_id(0)]

    def body(columns):
        cols = slice(0, columns)
        mean, inverse = first_norm((sa, sb, sc, sd), cols)
        normed = (resid[:, cols] - mean) * inverse
        hidden = (normed * vec[:, 3:4] + vec[:, 4:5]).astype(BF16)
        hid[:, cols] = hidden
        pre_act = nn(wup_t[...], hidden) + bup[:, 0:1]
        activated, gradient = gelu_pair(pre_act)
        activated = activated.astype(BF16)
        act[:, cols] = activated
        slope[:, cols] = gradient.astype(BF16)
        resid_two = hidden.astype(F32) + nn(wdown[...], activated) + vec[:, 5:6]
        two[:, cols] = resid_two
        grad = cot[:, cols].astype(F32) * live_row(length, columns) * vec[:, 6:7]
        stats[0:1, cols] = colsum(resid_two)
        stats[1:2, cols] = colsum(resid_two * resid_two)
        stats[2:3, cols] = colsum(grad)
        stats[3:4, cols] = colsum(grad * resid_two)

    for_length(length, body)


def feed_backward_kernel(
    first, has_earlier, lens, group, two, ta, tb, tc, td, cot, slope, resid, sa, sb, sc, sd,
    wdown_t, wup, vec, *rest,
):
    *_, out, gtwo, gpre, ghid, stats, sums, sums_up = rest
    length = lens[first + pl.program_id(0)]

    @pl.when(pl.program_id(0) == 0)
    def _():
        sums[...] = jnp.zeros_like(sums)
        sums_up[...] = jnp.zeros_like(sums_up)

    def body(columns):
        cols = slice(0, columns)
        total = ta[:, cols] + tb[:, cols] + tc[:, cols] + td[:, cols]
        mean_two = total[0:1] / D
        inverse_two = lax.rsqrt(total[1:2] / D - mean_two * mean_two + EPSILON)
        normed_two = (two[:, cols] - mean_two) * inverse_two
        live = live_row(length, columns)
        out[:, cols] = ((normed_two * vec[:, 6:7] + vec[:, 7:8]) * live).astype(BF16)
        if columns < SLOT:
            out[:, columns:] = jnp.zeros((out.shape[0], SLOT - columns), BF16)
        upstream = cot[:, cols].astype(F32) * live
        sums[0] += fold(upstream * normed_two)
        sums[1] += fold(upstream)
        plain = total[2:3] / D
        weighted = inverse_two * (total[3:4] - mean_two * total[2:3]) / D
        grad_two = (
            inverse_two * (upstream * vec[:, 6:7] - plain - normed_two * weighted)
        ).astype(BF16)
        gtwo[:, cols] = grad_two
        grad_two_wide = grad_two.astype(F32)
        sums[2] += fold(grad_two_wide)
        grad_pre = (nn(wdown_t[...], grad_two) * slope[:, cols].astype(F32)).astype(BF16)
        gpre[:, cols] = grad_pre
        sums_up[...] += fold(grad_pre.astype(F32))
        grad_hidden = (grad_two_wide + nn(wup[...], grad_pre)).astype(BF16)
        ghid[:, cols] = grad_hidden
        grad_hidden = grad_hidden.astype(F32)
        mean, inverse = first_norm((sa, sb, sc, sd), cols)
        normed = (resid[:, cols] - mean) * inverse
        sums[3] += fold(grad_hidden * normed)
        sums[4] += fold(grad_hidden)
        grad = grad_hidden * vec[:, 3:4]
        stats[0:1, cols] = colsum(grad)
        stats[1:2, cols] = colsum(grad * normed)

    for_length(length, body)


def residual_grad_kernel(
    first, lens, group, ghid, ua, ub, uc, ud, resid, sa, sb, sc, sd, vec, *rest
):
    *_, gone, sums = rest
    length = lens[first + pl.program_id(0)]

    @pl.when(pl.program_id(0) == 0)
    def _():
        sums[...] = jnp.zeros_like(sums)

    def body(columns):
        cols = slice(0, columns)
        mean, inverse = first_norm((sa, sb, sc, sd), cols)
        normed = (resid[:, cols] - mean) * inverse
        total = (ua[:, cols] + ub[:, cols] + uc[:, cols] + ud[:, cols]) / D
        grad = ghid[:, cols].astype(F32) * vec[:, 3:4]
        grad_one = (inverse * (grad - total[0:1] - normed * total[1:2])).astype(BF16)
        gone[:, cols] = grad_one
        sums[...] += fold(grad_one.astype(F32))

    for_length(length, body)


def weight_grad_kernel(
    first, last_chunk, lens, group, gtwo, act, hid, gpre, gone, ctx0, ctx1, ctx2, ctx3, sums,
    sums_out, sums_up, *rest,
):
    *earlier, packed, dwdown, dwup, dwo, small = rest
    step = pl.program_id(0)
    length = lens[first + step]
    width, units = dwdown.shape

    @pl.when(step == 0)
    def _():
        if earlier:
            before = earlier[0]
            dwdown[...] = before[:, :units]
            dwup[...] = before[:, units : 2 * units]
            for place in range(GROUPS):
                start = 2 * units + place * width
                dwo[place] = before[:, start : start + width]
            small[...] = before[:, 2 * units + GROUPS * width :]
        else:
            dwdown[...] = jnp.zeros_like(dwdown)
            dwup[...] = jnp.zeros_like(dwup)
            dwo[...] = jnp.zeros_like(dwo)
            small[...] = jnp.zeros_like(small)
        columns = [rowsum(sums[place]) for place in range(5)] + [rowsum(sums_out[...])]
        columns += [
            rowsum(sums_up[part * width : (part + 1) * width]) for part in range(units // width)
        ]
        for place, column in enumerate(columns):
            small[:, place : place + 1] += column

    def body(columns):
        cols = slice(0, columns)
        dwdown[...] += nt(gtwo[:, cols], act[:, cols])
        dwup[...] += nt(hid[:, cols], gpre[:, cols])
        for place, ctx in enumerate((ctx0, ctx1, ctx2, ctx3)):
            dwo[place] += nt(ctx[:, cols], gone[:, cols])

    for_length(length, body)

    @pl.when(step == pl.num_programs(0) - 1)
    def _():
        kind = packed.dtype
        packed[:, :units] = dwdown[...].astype(kind)
        packed[:, units : 2 * units] = dwup[...].astype(kind)
        for place in range(GROUPS):
            start = 2 * units + place * width
            packed[:, start : start + width] = dwo[place].astype(kind)
        packed[:, 2 * units + GROUPS * width :] = small[...].astype(kind)


def attend_backward_kernel(
    first, last_chunk, lens, group, g0, g1, g2, g3, qkv, lse, tok, wo, wqkv, *rest
):
    *earlier, gtok, packed, dwqkv, sums, gqkv = rest
    step = pl.program_id(0)
    length = lens[first + step]
    width = tok.shape[0]

    @pl.when(step == 0)
    def _():
        if first:
            before = earlier[0]
            dwqkv[...] = before[:, : 3 * width]
        else:
            dwqkv[...] = jnp.zeros_like(dwqkv)
        sums[...] = jnp.zeros_like(sums)

    def body(columns):
        cols = slice(0, columns)
        grad_context = nn(wo[0], g0[:, cols])
        for place, grad in ((1, g1), (2, g2), (3, g3)):
            grad_context = grad_context + nn(wo[place], grad[:, cols])
        grad_context = grad_context.astype(BF16)
        for head in range(width // HDIM):
            start = head * HDIM
            rows = slice(start, start + HDIM)
            query = qkv[rows, cols]
            key = qkv[width + start : width + start + HDIM, cols]
            value = qkv[2 * width + start : 2 * width + start + HDIM, cols]
            grad = grad_context[rows]
            scores = mask_keys(tn(key, query), length)
            probs = jnp.exp(scores - lse[head : head + 1, cols])
            grad_probs = tn(value, grad)
            inner = colsum(grad_probs * probs)
            grad_scores = (probs * (grad_probs - inner)).astype(BF16)
            gqkv[rows, cols] = (nn(key, grad_scores) * SCALE).astype(BF16)
            gqkv[width + start : width + start + HDIM, cols] = nt(query, grad_scores).astype(BF16)
            gqkv[2 * width + start : 2 * width + start + HDIM, cols] = nt(
                grad, probs.astype(BF16)
            ).astype(BF16)
        grad_proj = gqkv[:, cols]
        sums[0] += fold(grad_proj[:width].astype(F32))
        sums[1] += fold(grad_proj[2 * width :].astype(F32))
        dwqkv[...] += nt(tok[:, cols], grad_proj)
        gtok[:, cols] = (nn(wqkv[...], grad_proj) + g0[:, cols].astype(F32)).astype(BF16)
        if columns < SLOT:
            gtok[:, columns:] = jnp.zeros((width, SLOT - columns), BF16)

    for_length(length, body)

    @pl.when(step == pl.num_programs(0) - 1)
    def _():
        kind = packed.dtype
        tail = jnp.zeros((width, packed.shape[1] - 3 * width - 2), F32)
        small = jnp.concatenate([rowsum(sums[0]), rowsum(sums[1]), tail], axis=1)
        if first:
            small = small + earlier[0][:, 3 * width :]
        packed[:, : 3 * width] = dwqkv[...].astype(kind)
        packed[:, 3 * width :] = small.astype(kind)


def slots(rows, offset=0):
    return pl.BlockSpec((rows, SLOT), lambda i, lens, group: (0, i + offset))


def group_slots(rows, flip):
    return pl.BlockSpec((rows, SLOT), lambda i, lens, group: (group[0] ^ flip, i))


def whole(*shape):
    return pl.BlockSpec(shape, lambda i, lens, group: (0,) * len(shape))


def call(chain, kernel, name, count, scalars, ins, outs, scratch=(), aliases=None, us=0.0, vmem=24):
    body, after = kernel, list(chain)
    if after:
        place = len(scalars) + len(ins)
        ins = ins + [(array, pl.BlockSpec(memory_space=pl.ANY)) for array in after]

        def body(*refs):
            return kernel(*refs[:place], *refs[place + len(after) :])

    results = pl.pallas_call(
        body,
        out_shape=[jax.ShapeDtypeStruct(shape, kind) for shape, kind, _ in outs],
        grid_spec=pltpu.PrefetchScalarGridSpec(
            num_scalar_prefetch=len(scalars),
            grid=(count,),
            in_specs=[block for _, block in ins],
            out_specs=[block for _, _, block in outs],
            scratch_shapes=list(scratch),
        ),
        input_output_aliases=aliases or {},
        compiler_params=pltpu.CompilerParams(
            dimension_semantics=("arbitrary",), vmem_limit_bytes=vmem * 2**20
        ),
        cost_estimate=pl.CostEstimate(
            flops=int(us * COST * 1.1e9), bytes_accessed=0, transcendentals=0
        ),
        name=name,
    )(*scalars, *[array for array, _ in ins])
    chain[:] = [results[-1]]
    return results


def permute(array, flip):
    return lax.ppermute(array, "grp", [(g, g ^ flip) for g in range(GROUPS)])


def gather_wide(array, way):
    width = array.shape[0]
    if way == "gather":
        every = lax.all_gather(array, "grp", axis=0, tiled=True)
        return [(array, slots(width))] + [
            (every, group_slots(width, flip)) for flip in (1, 2, 3)
        ]
    return relay(array, permute(array, 1), permute(array, 2))


def relay(array, near, across):
    arrays = [array, near, across, permute(across, 1)]
    return [(a, slots(array.shape[0])) for a in arrays]


def gather_small(array):
    return [array] + [permute(array, flip) for flip in (1, 2, 3)]


def scatter_over_seq(packed):
    ranks = lax.axis_size("seq")
    rows, columns = packed.shape
    return lax.all_to_all(packed.reshape(ranks, rows // ranks, columns), "seq", 0, 0)


def sum_over_seq(chain, scalars, shares, held=None):
    ranks, rows, columns = shares.shape
    block = whole(ranks, rows, columns)
    ins, outs, aliases = [(shares, block)], [(shares.shape, BF16, block)], {}
    if held is not None:
        place = pl.BlockSpec(memory_space=pl.ANY)
        ins, outs = ins + [(held, place)], [(held.shape, held.dtype, place)] + outs
        aliases = {len(scalars) + 1: 0}
    *passed, own = call(
        chain, share_kernel, "share", 1, scalars, ins, outs, aliases=aliases, us=1.0
    )
    total = lax.all_to_all(own, "seq", 0, 0).reshape(ranks * rows, columns)
    return (total, *passed) if passed else total


def local(
    tokens, lengths, w_qkv, b_qv, w_out, b_out, ln1_gain, ln1_bias, w_up, b_up, w_down, b_down,
    ln2_gain, ln2_bias, cotangent,
):
    width, row_count = tokens.shape
    units = w_up.shape[1]
    seq_count = lengths.shape[0]
    group = lax.axis_index("grp").astype(jnp.int32)
    scalars = (lengths, group[None])
    parts = units // width
    rows = jnp.concatenate(
        [b_qv.reshape(-1), b_out, ln1_gain, ln1_bias, b_down, ln2_gain, ln2_bias, b_up]
    ).reshape(8 + parts, width)
    chain = []
    bounds = [seq_count * part // CHUNKS for part in range(CHUNKS + 1)]
    chunks = [(a, b - a) for a, b in zip(bounds[:-1], bounds[1:])]
    cubes = ((GROUPS, width, width), BF16, whole(GROUPS, width, width))
    wo, wo_t = call(
        chain, mixers_kernel, "mixers", 1, scalars, [(w_out, whole(width, D))], [cubes, cubes],
        scratch=[pltpu.VMEM((D, width), BF16)], vmem=60,
    )
    mixers = [wo_t[0]] + [permute(wo_t[flip], flip) for flip in (1, 2, 3)]
    forward = []
    for first, count in chunks:
        length = count * SLOT
        forward.append(
            call(
                chain, functools.partial(attend_forward_kernel, first), "attend_forward", count, scalars,
                [
                    (tokens, slots(width, first)), (w_qkv, whole(width, 3 * width)),
                    (b_qv, whole(2, width)),
                ],
                [
                    ((width, length), BF16, slots(width)),
                    ((3 * width, length), BF16, slots(3 * width)),
                    ((8, length), F32, slots(8)),
                ],
                scratch=[pltpu.VMEM((3 * width, width), BF16), pltpu.VMEM((width, 8), F32)],
                us=8.0, vmem=60,
            )
        )
        if first == 0:
            vec, bup, wup_t, wdown_t = call(
                chain, prepare_kernel, "prepare", 1, scalars,
                [
                    (rows, whole(8 + parts, width)), (w_up, whole(width, units)),
                    (w_down, whole(width, units)),
                ],
                [
                    ((width, 8 + parts), F32, whole(width, 8 + parts)),
                    ((units, 1), F32, whole(units, 1)),
                    ((units, width), BF16, whole(units, width)),
                    ((units, width), BF16, whole(units, width)),
                ],
                vmem=60,
            )
            chain += mixers[1:]
    vec_in, bup_in = (vec, whole(width, 8 + parts)), (bup, whole(units, 1))
    contexts = [gather_wide(f[0], way) for f, way in zip(forward, CONTEXT_WAYS)]
    mixed, normed, ups, backs, gones, gwide = [], [], [], [], [], []
    for (first, count), ctx in zip(chunks, contexts):
        rows = count * SLOT
        resid, stats = call(
            chain, functools.partial(mix_kernel, first), "mix", count, scalars,
            ctx + [(tokens, slots(width, first))] + [(m, whole(width, width)) for m in mixers]
            + [vec_in],
            [((width, rows), F32, slots(width)), ((2, rows), F32, slots(2))],
            us=3.0,
        )
        mixed.append((resid, stats))
        normed.append([(s, slots(2)) for s in gather_small(stats)])
    for (first, count), (resid, _), one in zip(chunks, mixed, normed):
        rows = count * SLOT
        ups.append(call(
            chain, functools.partial(feed_forward_kernel, first), "feed_forward", count, scalars,
            [(resid, slots(width))] + one + [
                (cotangent, slots(width, first)), (wup_t, whole(units, width)),
                (w_down, whole(width, units)), vec_in, bup_in,
            ],
            [
                ((width, rows), BF16, slots(width)),
                ((units, rows), BF16, slots(units)),
                ((units, rows), BF16, slots(units)),
                ((width, rows), F32, slots(width)),
                ((4, rows), F32, slots(4)),
            ],
            us=8.0,
        ))
    output = None
    for (first, count), (resid, _), one, up in zip(chunks, mixed, normed, ups):
        rows = count * SLOT
        hid, act, slope, two, stats = up
        ins = (
            [(two, slots(width))] + [(s, slots(4)) for s in gather_small(stats)] + [
                (cotangent, slots(width, first)), (slope, slots(units)), (resid, slots(width)),
            ] + one + [(wdown_t, whole(units, width)), (w_up, whole(width, units)), vec_in]
        )
        aliases = {}
        if output is not None:
            aliases = {len(scalars) + len(ins): 0}
            ins = ins + [(output, pl.BlockSpec(memory_space=pl.ANY))]
        output, gtwo, gpre, ghid, stats, sums, sums_up = call(
            chain, functools.partial(feed_backward_kernel, first, output is not None), "feed_backward",
            count, scalars, ins,
            [
                ((width, row_count), BF16, slots(width, first)),
                ((width, rows), BF16, slots(width)),
                ((units, rows), BF16, slots(units)),
                ((width, rows), BF16, slots(width)),
                ((2, rows), F32, slots(2)),
                ((5, width, LANE), F32, whole(5, width, LANE)),
                ((units, LANE), F32, whole(units, LANE)),
            ],
            aliases=aliases, us=8.0,
        )
        backs.append((gtwo, gpre, ghid, stats, sums, sums_up))
    for (first, count), (resid, _), one, back in zip(chunks, mixed, normed, backs):
        rows = count * SLOT
        gone, sums_out = call(
            chain, functools.partial(residual_grad_kernel, first), "residual_grad", count, scalars,
            [(back[2], slots(width))] + [(s, slots(2)) for s in gather_small(back[3])]
            + [(resid, slots(width))] + one + [vec_in],
            [((width, rows), BF16, slots(width)), ((width, LANE), F32, whole(width, LANE))],
            us=2.0,
        )
        gones.append((gone, sums_out))
    gwide = [gather_wide(gones[0][0], "permute"), None]
    late = gones[1][0], permute(gones[1][0], 1), permute(gones[1][0], 2)
    packed = None
    pack_width = 2 * units + GROUPS * width + LANE
    for (first, count), ctx, up, back, gone in zip(chunks, contexts, ups, backs, gones):
        final = first + count == seq_count
        hid, act = up[:2]
        gtwo, gpre, _, _, sums, sums_up = back
        ins = [
            (gtwo, slots(width)), (act, slots(units)), (hid, slots(width)), (gpre, slots(units)),
            (gone[0], slots(width)), *ctx, (sums, whole(5, width, LANE)),
            (gone[1], whole(width, LANE)), (sums_up, whole(units, LANE)),
        ]
        if packed is not None:
            ins.append((packed, whole(width, pack_width)))
        (packed,) = call(
            chain, functools.partial(weight_grad_kernel, first, final), "weight_grad", count, scalars,
            ins,
            [((width, pack_width), BF16 if final else F32, whole(width, pack_width))],
            scratch=[
                pltpu.VMEM((width, units), F32), pltpu.VMEM((width, units), F32),
                pltpu.VMEM((GROUPS, width, width), F32), pltpu.VMEM((width, LANE), F32),
            ],
            us=25.0,
        )
    weight_shares = scatter_over_seq(packed)
    grad_tokens, packed_qkv = None, None
    qkv_width = 3 * width + LANE // 2
    for (first, count), gone, (_, qkv, lse) in zip(chunks, gwide, forward):
        final = first + count == seq_count
        if final:
            weight_sums, across = sum_over_seq(chain, scalars, weight_shares, late[2])
            gone = relay(*late[:2], across)
        ins = [
            *gone, (qkv, slots(3 * width)), (lse, slots(8)), (tokens, slots(width, first)),
            (wo, whole(GROUPS, width, width)), (w_qkv, whole(width, 3 * width)),
        ]
        aliases = {}
        if first:
            ins.append((packed_qkv, whole(width, qkv_width)))
            aliases = {len(scalars) + len(ins): 0}
            ins.append((grad_tokens, pl.BlockSpec(memory_space=pl.ANY)))
        grad_tokens, packed_qkv = call(
            chain, functools.partial(attend_backward_kernel, first, final), "attend_backward", count,
            scalars, ins,
            [
                ((width, row_count), BF16, slots(width, first)),
                ((width, qkv_width), BF16 if final else F32, whole(width, qkv_width)),
            ],
            scratch=[
                pltpu.VMEM((width, 3 * width), F32), pltpu.VMEM((2, width, LANE), F32),
                pltpu.VMEM((3 * width, SLOT), BF16),
            ],
            aliases=aliases, us=14.0, vmem=60,
        )
    chain.append(weight_sums)
    qkv_sums = sum_over_seq(chain, scalars, scatter_over_seq(packed_qkv))
    routed = [weight_sums[:, 2 * units + r * width : 2 * units + (r + 1) * width] for r in range(4)]
    routed = jnp.stack([routed[0]] + [permute(routed[flip], flip) for flip in (1, 2, 3)])
    grad_w_out = jnp.concatenate(
        [lax.dynamic_index_in_dim(routed, group ^ t, 0, False) for t in range(GROUPS)], axis=1
    ).astype(F32)
    small = weight_sums[:, 2 * units + GROUPS * width :][:, : 6 + parts].T.astype(F32)
    small_qv = qkv_sums[:, 3 * width :][:, :2].T.astype(F32)
    return (
        output, grad_tokens, qkv_sums[:, : 3 * width].astype(F32), small_qv, grad_w_out, small[5],
        small[3], small[4], weight_sums[:, units : 2 * units].astype(F32),
        small[6:].reshape(-1), weight_sums[:, :units].astype(F32), small[2], small[0], small[1],
    )


def solution(mesh):
    row, vector = P("grp", None), P("grp")
    placed = (
        P("grp", "seq"), P("seq"), row, P(None, "grp"), row, vector, vector, vector, row, vector,
        row, vector, vector, vector, P("grp", "seq"),
    )
    results = (
        P("grp", "seq"), P("grp", "seq"), row, P(None, "grp"), row, vector, vector, vector, row,
        vector, row, vector, vector, vector,
    )
    return jax.shard_map(local, mesh=mesh, in_specs=placed, out_specs=results, check_vma=False)
```

```python
import functools
import math

import jax
import jax.numpy as jnp
from jax import lax
from jax.experimental import pallas as pl
from jax.experimental.pallas import tpu as pltpu
from jax.sharding import PartitionSpec as P

D = 768
HDIM = 64
SLOT = 512
LANE = 128
GROUPS = 4
EPSILON = 1e-06
MASKED_SCORE = -1000000000.0
SCALE = 1.0 / math.sqrt(HDIM)
FIRST_CHUNK = 0.5
ORDER = ("A0", "P0", "A1", "H0", "M0", "H1", "M1", "U0", "U1", "B0", "B1", "T0", "R0", "R1", "W0", "W1", "G0", "D0", "S1", "D1")
WEIGHT_US = 8.0, 8.0
BACKWARD_US = 4.0, 100.0
ATTEND_US = 8.0
MIDDLE_US = 1.0
CONTEXT_WAYS = "permute", "permute"
CONTEXT_HELD = ()
GRADIENT_WAYS = "permute", "permute"
GRADIENT_HELD = (1,)
VMEM = 60
MID_VMEM = 16
COST = 1.0
F32 = jnp.float32
BF16 = jnp.bfloat16


def nn(left, right):
    return lax.dot_general(left, right, (((1,), (0,)), ((), ())), preferred_element_type=F32)


def tn(left, right):
    return lax.dot_general(left, right, (((0,), (0,)), ((), ())), preferred_element_type=F32)


def nt(left, right):
    return lax.dot_general(left, right, (((1,), (1,)), ((), ())), preferred_element_type=F32)


def for_length(length, body):
    blocks = (length + (LANE - 1)) // LANE
    for count in range(1, SLOT // LANE + 1):
        pl.when(blocks == count)(functools.partial(body, count * LANE))


def fold(array):
    total = array[:, :LANE]
    for start in range(LANE, array.shape[1], LANE):
        total = total + array[:, start : start + LANE]
    return total


def live_row(length, columns):
    return (lax.broadcasted_iota(jnp.int32, (1, columns), 1) < length).astype(F32)


def mask_keys(scores, length):
    columns = scores.shape[0]
    start = columns - LANE
    last = scores[start:]
    key = lax.broadcasted_iota(jnp.int32, last.shape, 0) + start
    last = jnp.where(key < length, last, MASKED_SCORE)
    return last if start == 0 else jnp.concatenate([scores[:start], last], axis=0)


def normal(values):
    return 0.5 + 0.5 * lax.erf(values * 0.7071067811865476)


def colsum(array):
    return jnp.sum(array, axis=0, keepdims=True)


def rowsum(array):
    return jnp.sum(array, axis=1, keepdims=True)


def hold_kernel(lens, group, *refs):
    pass


def prepare_kernel(lens, group, rows, w_out, w_up, w_down, vec, bup, wo, wo_t, wup_t, wdown_t, flat):
    width = w_out.shape[0]
    flat[...] = jnp.transpose(w_out[...])
    for flip in range(GROUPS):
        block = flat[pl.ds(pl.multiple_of((group[0] ^ flip) * width, width), width), :]
        wo[flip] = jnp.transpose(block)
        if flip < 2:
            wo_t[flip] = block
    vectors = jnp.transpose(rows[...].astype(F32))
    vec[...] = vectors
    for part in range(bup.shape[0] // width):
        bup[part * width : (part + 1) * width, :] = vectors[:, 8 + part : 9 + part]
    wup_t[...] = jnp.transpose(w_up[...])
    wdown_t[...] = jnp.transpose(w_down[...])


def share_kernel(lens, group, shares, *rest):
    own = rest[-1]
    total = shares[0].astype(F32)
    for place in range(1, shares.shape[0]):
        total = total + shares[place].astype(F32)
    own[...] = jnp.broadcast_to(total.astype(BF16)[None], own.shape)


def attend_forward_kernel(
    first, count, lens, group, tok, wqkv, bias, w_out, ctx, qkv, lse, wqkv_t, cols_qv, flat
):
    step = pl.program_id(0)
    width = tok.shape[0]

    @pl.when(step == count)
    def _():
        flat[...] = jnp.transpose(w_out[...])
        for place, flip in ((0, 2), (SLOT // 2, 3)):
            start = pl.multiple_of((group[0] ^ flip) * width, width)
            ctx[:, place : place + width] = flat[pl.ds(start, width), :]

    @pl.when(step < count)
    def _():
        attend_forward_step(
            lens[first + jnp.minimum(step, count - 1)], tok, wqkv, bias, ctx, qkv, lse, wqkv_t, cols_qv
        )


def attend_forward_step(length, tok, wqkv, bias, ctx, qkv, lse, wqkv_t, cols_qv):
    width = tok.shape[0]

    @pl.when(pl.program_id(0) == 0)
    def _():
        wqkv_t[...] = jnp.transpose(wqkv[...])
        cols_qv[...] = jnp.transpose(jnp.concatenate([bias[...].astype(F32)] * 4, axis=0))

    def body(columns):
        cols = slice(0, columns)
        proj = nn(wqkv_t[...], tok[:, cols])
        query = ((proj[:width] + cols_qv[:, 0:1]) * SCALE).astype(BF16)
        key = proj[width : 2 * width].astype(BF16)
        value = (proj[2 * width :] + cols_qv[:, 1:2]).astype(BF16)
        qkv[:width, cols] = query
        qkv[width : 2 * width, cols] = key
        qkv[2 * width :, cols] = value
        for head in range(width // HDIM):
            rows = slice(head * HDIM, (head + 1) * HDIM)
            scores = mask_keys(tn(key[rows], query[rows]), length)
            highest = jnp.max(scores, axis=0, keepdims=True)
            weights = jnp.exp(scores - highest)
            total = colsum(weights)
            ctx[rows, cols] = (nn(value[rows], weights.astype(BF16)) * (1.0 / total)).astype(BF16)
            lse[head : head + 1, cols] = highest + jnp.log(total)
        if columns < SLOT:
            ctx[:, columns:] = jnp.zeros((width, SLOT - columns), BF16)

    for_length(length, body)


def mix_kernel(
    first, lens, group, ctx0, ctx1, ctx2, ctx3, tok, wo0, wo1, wo2, wo3, vec, resid, stats
):
    length = lens[first + pl.program_id(0)]

    def body(columns):
        cols = slice(0, columns)
        total = tok[:, cols].astype(F32) + vec[:, 2:3]
        width = tok.shape[0]
        mixers = (
            wo0[...], wo1[...], wo2[:, :width], wo3[:, SLOT // 2 : SLOT // 2 + width]
        )
        for mixer, context in zip(mixers, (ctx0, ctx1, ctx2, ctx3)):
            total = total + nn(mixer, context[:, cols])
        resid[:, cols] = total
        stats[0:1, cols] = colsum(total)
        stats[1:2, cols] = colsum(total * total)

    for_length(length, body)


def first_norm(stats, cols):
    total = stats[0][:, cols] + stats[1][:, cols] + stats[2][:, cols]
    mean = total[0:1] / D
    inverse = lax.rsqrt(total[1:2] / D - mean * mean + EPSILON)
    return mean, inverse


def feed_forward_kernel(
    first, lens, group, resid, sa, sb, sc, cot, wup_t, wdown, vec, bup, hid, two, stats
):
    length = lens[first + pl.program_id(0)]

    def body(columns):
        cols = slice(0, columns)
        mean, inverse = first_norm((sa, sb, sc), cols)
        normed = (resid[:, cols] - mean) * inverse
        hidden = (normed * vec[:, 3:4] + vec[:, 4:5]).astype(BF16)
        hid[:, cols] = hidden
        pre_act = nn(wup_t[...], hidden) + bup[:, 0:1]
        activated = (pre_act * normal(pre_act)).astype(BF16)
        resid_two = hidden.astype(F32) + nn(wdown[...], activated) + vec[:, 5:6]
        two[:, cols] = resid_two
        grad = cot[:, cols].astype(F32) * live_row(length, columns) * vec[:, 6:7]
        stats[0:1, cols] = colsum(resid_two)
        stats[1:2, cols] = colsum(resid_two * resid_two)
        stats[2:3, cols] = colsum(grad)
        stats[3:4, cols] = colsum(grad * resid_two)

    for_length(length, body)


def feed_backward_kernel(
    first, has_earlier, lens, group, two, ta, tb, tc, cot, hid, resid, sa, sb, sc, wup_t, wdown_t,
    wup, vec, bup, *rest,
):
    *earlier, out, ghid, stats, grads, sums, sums_up = rest
    step = pl.program_id(0)
    length = lens[first + step]
    width, units = wup.shape

    @pl.when(step == 0)
    def _():
        grads[...] = earlier[0][...] if has_earlier else jnp.zeros_like(grads)
        sums[...] = jnp.zeros_like(sums)
        sums_up[...] = jnp.zeros_like(sums_up)

    def body(columns):
        cols = slice(0, columns)
        hidden = hid[:, cols]
        pre_act = nn(wup_t[...], hidden) + bup[:, 0:1]
        total = ta[:, cols] + tb[:, cols] + tc[:, cols]
        mean_two = total[0:1] / D
        inverse_two = lax.rsqrt(total[1:2] / D - mean_two * mean_two + EPSILON)
        normed_two = (two[:, cols] - mean_two) * inverse_two
        live = live_row(length, columns)
        out[:, cols] = ((normed_two * vec[:, 6:7] + vec[:, 7:8]) * live).astype(BF16)
        if columns < SLOT:
            out[:, columns:] = jnp.zeros((width, SLOT - columns), BF16)
        upstream = cot[:, cols].astype(F32) * live
        sums[0] += fold(upstream * normed_two)
        sums[1] += fold(upstream)
        plain = total[2:3] / D
        weighted = inverse_two * (total[3:4] - mean_two * total[2:3]) / D
        grad_two = (
            inverse_two * (upstream * vec[:, 6:7] - plain - normed_two * weighted)
        ).astype(BF16)
        grad_two_wide = grad_two.astype(F32)
        sums[2] += fold(grad_two_wide)
        grad_act = nn(wdown_t[...], grad_two)
        normal_cdf = normal(pre_act)
        activated = (pre_act * normal_cdf).astype(BF16)
        slope = normal_cdf + pre_act * (0.3989422804014327 * jnp.exp(-0.5 * pre_act * pre_act))
        grad_pre = (grad_act * slope).astype(BF16)
        sums_up[...] += fold(grad_pre.astype(F32))
        grad_hidden = (grad_two_wide + nn(wup[...], grad_pre)).astype(BF16)
        ghid[:, cols] = grad_hidden
        grads[:, :units] += nt(grad_two, activated)
        grads[:, units : 2 * units] += nt(hidden, grad_pre)
        grad_hidden = grad_hidden.astype(F32)
        mean, inverse = first_norm((sa, sb, sc), cols)
        normed = (resid[:, cols] - mean) * inverse
        sums[3] += fold(grad_hidden * normed)
        sums[4] += fold(grad_hidden)
        grad = grad_hidden * vec[:, 3:4]
        stats[0:1, cols] = colsum(grad)
        stats[1:2, cols] = colsum(grad * normed)

    for_length(length, body)

    @pl.when(step == pl.num_programs(0) - 1)
    def _():
        columns = [rowsum(sums[place]) for place in range(5)] + [jnp.zeros((width, 1), F32)]
        columns += [
            rowsum(sums_up[part * width : (part + 1) * width]) for part in range(units // width)
        ]
        for place, column in enumerate(columns):
            grads[:, 2 * units + place : 2 * units + place + 1] += column


def residual_grad_kernel(
    first, lens, group, ghid, ua, ub, uc, resid, sa, sb, sc, vec, *rest
):
    *_, gone, sums = rest
    length = lens[first + pl.program_id(0)]

    @pl.when(pl.program_id(0) == 0)
    def _():
        sums[...] = jnp.zeros_like(sums)

    def body(columns):
        cols = slice(0, columns)
        mean, inverse = first_norm((sa, sb, sc), cols)
        normed = (resid[:, cols] - mean) * inverse
        total = (ua[:, cols] + ub[:, cols] + uc[:, cols]) / D
        grad = ghid[:, cols].astype(F32) * vec[:, 3:4]
        grad_one = (inverse * (grad - total[0:1] - normed * total[1:2])).astype(BF16)
        gone[:, cols] = grad_one
        sums[...] += fold(grad_one.astype(F32))

    for_length(length, body)


def weight_grad_kernel(first, lens, group, gone, ctx0, ctx1, ctx2, ctx3, sums_out, *rest):
    *earlier, packed, dwo = rest
    step = pl.program_id(0)
    length = lens[first + step]
    width = gone.shape[0]

    @pl.when(step == 0)
    def _():
        dwo[...] = earlier[0][...] if earlier else jnp.zeros_like(dwo)

    def body(columns):
        cols = slice(0, columns)
        for place, context in enumerate((ctx0, ctx1, ctx2, ctx3)):
            dwo[place] += nt(context[:, cols], gone[:, cols])

    for_length(length, body)

    @pl.when(step == pl.num_programs(0) - 1)
    def _():
        if not earlier:
            packed[...] = dwo[...]
            return
        _, grads, sums_first = earlier
        double = grads.shape[1] - LANE
        start = double + GROUPS * width
        packed[:, :double] = grads[:, :double].astype(BF16)
        for place in range(GROUPS):
            packed[:, double + place * width : double + (place + 1) * width] = dwo[place].astype(BF16)
        lane = lax.broadcasted_iota(jnp.int32, (width, LANE), 1)
        bias = rowsum(sums_out[...]) + rowsum(sums_first[...])
        packed[:, start:] = jnp.where(lane == 5, bias, grads[:, double:]).astype(BF16)


def unpack_kernel(lens, group, packed, d0, d1, d2, d3, small, dwup, dwdown):
    width, units = dwup.shape
    dwdown[...] = packed[:, :units].astype(F32)
    dwup[...] = packed[:, units : 2 * units].astype(F32)
    for place, block in enumerate((d0, d1, d2, d3)):
        start = 2 * units + place * width
        block[...] = packed[:, start : start + width]
    small[...] = jnp.transpose(packed[:, 2 * units + GROUPS * width :].astype(F32))


def assemble_kernel(lens, group, d0, d1, d2, d3, out, blocks):
    width = d0.shape[0]
    for place, block in enumerate((d0, d1, d2, d3)):
        blocks[place] = block[...].astype(F32)
    for place in range(GROUPS):
        out[:, place * width : (place + 1) * width] = blocks[group[0] ^ place]


def unpack_qkv_kernel(lens, group, packed, bias, dwqkv):
    columns = dwqkv.shape[1]
    dwqkv[...] = packed[:, :columns].astype(F32)
    small = packed[:, columns:].astype(F32)
    bias[...] = jnp.transpose(jnp.concatenate([small, small], axis=1))[:2]


def attend_backward_kernel(
    first, has_earlier, lens, group, g0, g1, g2, g3, qkv, lse, tok, wo, wqkv, *rest
):
    *earlier, gtok, packed, dwqkv, sums, gqkv = rest
    step = pl.program_id(0)
    length = lens[first + step]
    width = tok.shape[0]

    @pl.when(step == 0)
    def _():
        if has_earlier:
            before = earlier[0]
            dwqkv[...] = before[:, : 3 * width]
        else:
            dwqkv[...] = jnp.zeros_like(dwqkv)
        sums[...] = jnp.zeros_like(sums)

    def body(columns):
        cols = slice(0, columns)
        grad_context = nn(wo[0], g0[:, cols])
        for place, grad in ((1, g1), (2, g2), (3, g3)):
            grad_context = grad_context + nn(wo[place], grad[:, cols])
        grad_context = grad_context.astype(BF16)
        for head in range(width // HDIM):
            start = head * HDIM
            rows = slice(start, start + HDIM)
            query = qkv[rows, cols]
            key = qkv[width + start : width + start + HDIM, cols]
            value = qkv[2 * width + start : 2 * width + start + HDIM, cols]
            grad = grad_context[rows]
            scores = mask_keys(tn(key, query), length)
            probs = jnp.exp(scores - lse[head : head + 1, cols])
            grad_probs = tn(value, grad)
            inner = colsum(grad_probs * probs)
            grad_scores = (probs * (grad_probs - inner)).astype(BF16)
            gqkv[rows, cols] = (nn(key, grad_scores) * SCALE).astype(BF16)
            gqkv[width + start : width + start + HDIM, cols] = nt(query, grad_scores).astype(BF16)
            gqkv[2 * width + start : 2 * width + start + HDIM, cols] = nt(
                grad, probs.astype(BF16)
            ).astype(BF16)
        grad_proj = gqkv[:, cols]
        sums[0] += fold(grad_proj[:width].astype(F32))
        sums[1] += fold(grad_proj[2 * width :].astype(F32))
        dwqkv[...] += nt(tok[:, cols], grad_proj)
        gtok[:, cols] = (nn(wqkv[...], grad_proj) + g0[:, cols].astype(F32)).astype(BF16)
        if columns < SLOT:
            gtok[:, columns:] = jnp.zeros((width, SLOT - columns), BF16)

    for_length(length, body)

    @pl.when(step == pl.num_programs(0) - 1)
    def _():
        kind = packed.dtype
        tail = jnp.zeros((width, packed.shape[1] - 3 * width - 2), F32)
        small = jnp.concatenate([rowsum(sums[0]), rowsum(sums[1]), tail], axis=1)
        if has_earlier:
            small = small + earlier[0][:, 3 * width :]
        packed[:, : 3 * width] = dwqkv[...].astype(kind)
        packed[:, 3 * width :] = small.astype(kind)


def columns_of(rows, offset=0):
    return pl.BlockSpec((rows, SLOT), lambda i, lens, group: (0, i + offset))


def slots(rows):
    return pl.BlockSpec((None, rows, SLOT), lambda i, lens, group: (i, 0, 0))


def slot_at(place, rows):
    return pl.BlockSpec((None, rows, SLOT), lambda i, lens, group: (place, 0, 0))


def group_slots(rows, flip, count):
    return pl.BlockSpec(
        (None, rows, SLOT), lambda i, lens, group: ((group[0] ^ flip) * count + i, 0, 0)
    )


def whole(*shape):
    return pl.BlockSpec(shape, lambda i, lens, group: (0,) * len(shape))


def call(chain, kernel, name, count, scalars, ins, outs, scratch=(), aliases=None, us=0.0, vmem=None):
    body, after = kernel, list(chain)
    if after:
        place = len(scalars) + len(ins)
        ins = ins + [(array, pl.BlockSpec(memory_space=pl.ANY)) for array in after]

        def body(*refs):
            return kernel(*refs[:place], *refs[place + len(after) :])

    results = pl.pallas_call(
        body,
        out_shape=[jax.ShapeDtypeStruct(shape, kind) for shape, kind, _ in outs],
        grid_spec=pltpu.PrefetchScalarGridSpec(
            num_scalar_prefetch=len(scalars),
            grid=(count,),
            in_specs=[block for _, block in ins],
            out_specs=[block for _, _, block in outs],
            scratch_shapes=list(scratch),
        ),
        input_output_aliases=aliases or {},
        compiler_params=pltpu.CompilerParams(
            dimension_semantics=("arbitrary",), vmem_limit_bytes=(vmem or MID_VMEM) * 2**20
        ),
        cost_estimate=pl.CostEstimate(
            flops=int(us * COST * 1.1e9), bytes_accessed=0, transcendentals=0
        ),
        name=name,
    )(*scalars, *[array for array, _ in ins])
    chain[:] = [results[-1]]
    return results


def permute(array, flip):
    return lax.ppermute(array, "grp", [(g, g ^ flip) for g in range(GROUPS)])


def send_wide(array, way):
    if way == "gather":
        return [array, lax.all_gather(array, "grp", axis=0, tiled=True)]
    return [array, permute(array, 1), permute(array, 2)]


def spread_wide(array, *others):
    count, rows, _ = array.shape
    if len(others) == 1:
        return [(array, slots(rows))] + [
            (others[0], group_slots(rows, flip, count)) for flip in (1, 2, 3)
        ]
    near, across = others
    return [(a, slots(rows)) for a in (array, near, across, permute(across, 1))]


def gather_small(array):
    near = permute(array, 1)
    return [(a, slots(array.shape[1])) for a in (array, near, permute(array + near, 2))]


def scatter_over_seq(packed):
    ranks = lax.axis_size("seq")
    rows, columns = packed.shape
    return lax.all_to_all(packed.reshape(ranks, rows // ranks, columns), "seq", 0, 0)


def sum_over_seq(chain, scalars, shares, held=()):
    ranks, rows, columns = shares.shape
    block = whole(ranks, rows, columns)
    place = pl.BlockSpec(memory_space=pl.ANY)
    *passed, own = call(
        chain, share_kernel, "share", 1, scalars, [(shares, block)] + [(h, place) for h in held],
        [(h.shape, h.dtype, place) for h in held] + [(shares.shape, BF16, block)],
        aliases={len(scalars) + 1 + n: n for n in range(len(held))}, us=1.0,
    )
    return lax.all_to_all(own, "seq", 0, 0).reshape(ranks * rows, columns), passed


def hold(chain, scalars, arrays):
    place = pl.BlockSpec(memory_space=pl.ANY)
    return call(
        chain, hold_kernel, "hold", 1, scalars, [(a, place) for a in arrays],
        [(a.shape, a.dtype, place) for a in arrays],
        aliases={len(scalars) + n: n for n in range(len(arrays))},
    )


def local(
    tokens, lengths, w_qkv, b_qv, w_out, b_out, ln1_gain, ln1_bias, w_up, b_up, w_down, b_down,
    ln2_gain, ln2_bias, cotangent,
):
    width, row_count = tokens.shape
    units = w_up.shape[1]
    seq_count = lengths.shape[0]
    group = lax.axis_index("grp").astype(jnp.int32)
    scalars = (lengths, group[None])
    parts = units // width
    rows = jnp.concatenate(
        [b_qv.reshape(-1), b_out, ln1_gain, ln1_bias, b_down, ln2_gain, ln2_bias, b_up]
    ).reshape(8 + parts, width)
    chain = []
    middle = int(seq_count * FIRST_CHUNK)
    chunks = [(0, middle), (middle, seq_count - middle)]
    untouched = pl.BlockSpec(memory_space=pl.ANY)
    state = [{}, {}]
    shared = dict(output=None, grad_tokens=None, packed=None, packed_qkv=None)
    pack_width = 2 * units + GROUPS * width + LANE
    qkv_width = 3 * width + LANE // 2
    square = ((width, width), BF16, whole(width, width))

    def prepare(_):
        turned = ((units, width), BF16, whole(units, width))
        shared["vec"], shared["bup"], shared["wo"], wo_t, shared["wup_t"], shared["wdown_t"] = call(
            chain, prepare_kernel, "prepare", 1, scalars,
            [
                (rows, whole(8 + parts, width)), (w_out, whole(width, D)),
                (w_up, whole(width, units)), (w_down, whole(width, units)),
            ],
            [
                ((width, 8 + parts), F32, whole(width, 8 + parts)),
                ((units, 1), F32, whole(units, 1)),
                ((GROUPS, width, width), BF16, whole(GROUPS, width, width)),
                ((2, width, width), BF16, whole(2, width, width)), turned, turned,
            ],
            scratch=[pltpu.VMEM((D, width), BF16)], vmem=VMEM,
        )
        shared["mixers"] = [
            (wo_t, pl.BlockSpec((None, width, width), lambda i, lens, group: (0, 0, 0))),
            (permute(wo_t[1], 1), whole(width, width)),
        ]

    def attend(which):
        first, count = chunks[which]
        steps = count + 1 if which == 0 else count
        near_end = lambda i, lens, group: (0, first + jnp.minimum(i, count - 1))
        held = lambda height: pl.BlockSpec(
            (None, height, SLOT), lambda i, lens, group: (jnp.minimum(i, count - 1), 0, 0)
        )
        context, qkv, lse = call(
            chain, functools.partial(attend_forward_kernel, first, count), "attend_forward", steps,
            scalars,
            [
                (tokens, pl.BlockSpec((width, SLOT), near_end)), (w_qkv, whole(width, 3 * width)),
                (b_qv, whole(2, width)), (w_out, whole(width, D)),
            ],
            [
                ((steps, width, SLOT), BF16, slots(width)),
                ((count, 3 * width, SLOT), BF16, held(3 * width)),
                ((count, 8, SLOT), F32, held(8)),
            ],
            scratch=[
                pltpu.VMEM((3 * width, width), BF16), pltpu.VMEM((width, 8), F32),
                pltpu.VMEM((D, width), BF16),
            ],
            us=ATTEND_US, vmem=VMEM,
        )
        state[which].update(context=send_wide(context, CONTEXT_WAYS[which]), qkv=qkv, lse=lse)

    def hold_context(which):
        mine = state[which]
        if CONTEXT_WAYS[which] == "permute" and which in CONTEXT_HELD:
            mine["context"][2:] = hold(chain, scalars, mine["context"][2:])
        mine["contexts"] = spread_wide(*mine["context"])
        if which == 0:
            place = chunks[0][1]
            shared["mixers"] += [
                (array, slot_at(place, width)) for array, _ in mine["contexts"][2:]
            ]

    def mix(which):
        (first, count), mine = chunks[which], state[which]
        mine["resid"], stats = call(
            chain, functools.partial(mix_kernel, first), "mix", count, scalars,
            mine["contexts"] + [(tokens, columns_of(width, first))] + shared["mixers"]
            + [(shared["vec"], whole(width, 8 + parts))],
            [((count, width, SLOT), F32, slots(width)), ((count, 2, SLOT), F32, slots(2))],
            us=3.0 * MIDDLE_US,
        )
        mine["one"] = gather_small(stats)

    def feed_forward(which):
        (first, count), mine = chunks[which], state[which]
        mine["hid"], mine["two"], stats = call(
            chain, functools.partial(feed_forward_kernel, first), "feed_forward", count, scalars,
            [(mine["resid"], slots(width))] + mine["one"] + [
                (cotangent, columns_of(width, first)), (shared["wup_t"], whole(units, width)),
                (w_down, whole(width, units)), (shared["vec"], whole(width, 8 + parts)),
                (shared["bup"], whole(units, 1)),
            ],
            [
                ((count, width, SLOT), BF16, slots(width)),
                ((count, width, SLOT), F32, slots(width)),
                ((count, 4, SLOT), F32, slots(4)),
            ],
            us=8.0 * MIDDLE_US,
        )
        mine["second"] = gather_small(stats)

    def feed_backward(which):
        (first, count), mine = chunks[which], state[which]
        grads = ((width, 2 * units + LANE), F32, whole(width, 2 * units + LANE))
        ins = [(mine["two"], slots(width))] + mine["second"] + [
            (cotangent, columns_of(width, first)), (mine["hid"], slots(width)),
            (mine["resid"], slots(width)),
        ] + mine["one"] + [
            (shared["wup_t"], whole(units, width)), (shared["wdown_t"], whole(units, width)),
            (w_up, whole(width, units)), (shared["vec"], whole(width, 8 + parts)),
            (shared["bup"], whole(units, 1)),
        ]
        aliases, has_earlier = {}, shared["output"] is not None
        if has_earlier:
            ins.append((shared["grads"], grads[2]))
            aliases = {len(scalars) + len(ins): 0}
            ins.append((shared["output"], untouched))
        shared["output"], mine["ghid"], stats, shared["grads"] = call(
            chain, functools.partial(feed_backward_kernel, first, has_earlier), "feed_backward",
            count, scalars, ins,
            [
                ((width, row_count), BF16, columns_of(width, first)),
                ((count, width, SLOT), BF16, slots(width)),
                ((count, 2, SLOT), F32, slots(2)), grads,
            ],
            scratch=[pltpu.VMEM((5, width, LANE), F32), pltpu.VMEM((units, LANE), F32)],
            aliases=aliases, us=8.0 * MIDDLE_US,
        )
        mine["third"] = gather_small(stats)

    def wait_third(_):
        chain.extend(state[which]["third"][2][0] for which in (0, 1))

    def residual_grad(which):
        (first, count), mine = chunks[which], state[which]
        gone, mine["out"] = call(
            chain, functools.partial(residual_grad_kernel, first), "residual_grad", count, scalars,
            [(mine["ghid"], slots(width))] + mine["third"] + [(mine["resid"], slots(width))]
            + mine["one"] + [(shared["vec"], whole(width, 8 + parts))],
            [((count, width, SLOT), BF16, slots(width)), ((width, LANE), F32, whole(width, LANE))],
            us=2.0 * MIDDLE_US,
        )
        mine["gone"] = send_wide(gone, GRADIENT_WAYS[which])

    def weight_grad(which):
        (first, count), mine = chunks[which], state[which]
        final = shared["packed"] is not None
        ins = [
            (mine["gone"][0], slots(width)), *mine["contexts"], (mine["out"], whole(width, LANE)),
        ]
        result = ((GROUPS, width, width), F32, whole(GROUPS, width, width))
        if final:
            ins += [
                (shared["packed"], result[2]),
                (shared["grads"], whole(width, 2 * units + LANE)),
                (state[1 - which]["out"], whole(width, LANE)),
            ]
            result = ((width, pack_width), BF16, whole(width, pack_width))
        (shared["packed"],) = call(
            chain, functools.partial(weight_grad_kernel, first), "weight_grad", count, scalars, ins,
            [result], scratch=[pltpu.VMEM((GROUPS, width, width), F32)], us=WEIGHT_US[final],
        )
        if final:
            shared["shares"] = scatter_over_seq(shared["packed"])

    def share(which):
        mine = state[which]
        shared["weight_sums"], far = sum_over_seq(
            chain, scalars, shared["shares"], mine["gone"][2:] if which in GRADIENT_HELD else ()
        )
        if far:
            mine["gone"][2:] = far

    def hold_gone(which):
        mine = state[which]
        mine["gone"][2:] = hold(chain, scalars, mine["gone"][2:])

    def attend_backward(which):
        (first, count), mine = chunks[which], state[which]
        final = shared["packed_qkv"] is not None
        ins = [
            *spread_wide(*mine["gone"]), (mine["qkv"], slots(3 * width)), (mine["lse"], slots(8)),
            (tokens, columns_of(width, first)), (shared["wo"], whole(GROUPS, width, width)),
            (w_qkv, whole(width, 3 * width)),
        ]
        aliases = {}
        if final:
            ins.append((shared["packed_qkv"], whole(width, qkv_width)))
            aliases = {len(scalars) + len(ins): 0}
            ins.append((shared["grad_tokens"], untouched))
        shared["grad_tokens"], shared["packed_qkv"] = call(
            chain, functools.partial(attend_backward_kernel, first, final), "attend_backward", count,
            scalars, ins,
            [
                ((width, row_count), BF16, columns_of(width, first)),
                ((width, qkv_width), BF16 if final else F32, whole(width, qkv_width)),
            ],
            scratch=[
                pltpu.VMEM((width, 3 * width), F32), pltpu.VMEM((2, width, LANE), F32),
                pltpu.VMEM((3 * width, SLOT), BF16),
            ],
            aliases=aliases, us=BACKWARD_US[final], vmem=VMEM,
        )

    stages = dict(
        P=prepare, A=attend, H=hold_context, M=mix, U=feed_forward, B=feed_backward, R=residual_grad,
        T=wait_third, W=weight_grad, S=share, G=hold_gone, D=attend_backward,
    )
    for stage in ORDER:
        stages[stage[0]](int(stage[1]))
    output, grad_tokens = shared["output"], shared["grad_tokens"]
    shares_qkv = scatter_over_seq(shared["packed_qkv"])
    *blocks, small, grad_w_up, grad_w_down = call(
        chain, unpack_kernel, "unpack", 1, scalars,
        [(shared["weight_sums"], whole(width, pack_width))],
        [
            square, square, square, square,
            ((LANE, width), F32, whole(LANE, width)),
            ((width, units), F32, whole(width, units)),
            ((width, units), F32, whole(width, units)),
        ],
        us=3.0,
    )
    qkv_sums, _ = sum_over_seq(chain, scalars, shares_qkv)
    routed = [blocks[0]] + [permute(blocks[flip], flip) for flip in (1, 2, 3)]
    (grad_w_out,) = call(
        chain, assemble_kernel, "assemble", 1, scalars,
        [(block, whole(width, width)) for block in routed],
        [((width, D), F32, whole(width, D))],
        scratch=[pltpu.VMEM((GROUPS, width, width), F32)], us=1.0,
    )
    grad_b_qv, grad_w_qkv = call(
        chain, unpack_qkv_kernel, "unpack_qkv", 1, scalars, [(qkv_sums, whole(width, qkv_width))],
        [((2, width), F32, whole(2, width)), ((width, 3 * width), F32, whole(width, 3 * width))],
    )
    return (
        output, grad_tokens, grad_w_qkv, grad_b_qv, grad_w_out, small[5], small[3], small[4],
        grad_w_up, small[6 : 6 + parts].reshape(-1), grad_w_down, small[2], small[0], small[1],
    )


def solution(mesh):
    row, vector = P("grp", None), P("grp")
    placed = (
        P("grp", "seq"), P("seq"), row, P(None, "grp"), row, vector, vector, vector, row, vector,
        row, vector, vector, vector, P("grp", "seq"),
    )
    results = (
        P("grp", "seq"), P("grp", "seq"), row, P(None, "grp"), row, vector, vector, vector, row,
        vector, row, vector, vector, vector,
    )
    return jax.shard_map(local, mesh=mesh, in_specs=placed, out_specs=results, check_vma=False)
```

```python
import functools
import math

import jax
import jax.numpy as jnp
from jax import lax
from jax.experimental import pallas as pl
from jax.experimental.pallas import tpu as pltpu
from jax.sharding import PartitionSpec as P

D = 768
HDIM = 64
SLOT = 512
LANE = 128
GROUPS = 4
EPSILON = 1e-06
MASKED_SCORE = -1000000000.0
SCALE = 1.0 / math.sqrt(HDIM)
FIRST_CHUNK = 0.5
ORDER = ("A0", "P0", "A1", "H0", "M0", "H1", "M1", "U0", "U1", "B0", "B1", "T0", "R0", "R1", "W0", "W1", "G0", "D0", "S1", "D1")
WEIGHT_US = 8.0, 8.0
BACKWARD_US = 4.0, 100.0
ATTEND_US = 8.0
MIDDLE_US = 1.0
CONTEXT_WAYS = "permute", "permute"
CONTEXT_HELD = ()
GRADIENT_WAYS = "permute", "permute"
GRADIENT_HELD = (1,)
VMEM = 60
ATTEND_VMEM = 60, 20
BACKWARD_VMEM = 20, 20
MID_VMEM = 16
COST = 1.0
F32 = jnp.float32
BF16 = jnp.bfloat16


def nn(left, right):
    return lax.dot_general(left, right, (((1,), (0,)), ((), ())), preferred_element_type=F32)


def tn(left, right):
    return lax.dot_general(left, right, (((0,), (0,)), ((), ())), preferred_element_type=F32)


def nt(left, right):
    return lax.dot_general(left, right, (((1,), (1,)), ((), ())), preferred_element_type=F32)


def for_length(length, body):
    blocks = (length + (LANE - 1)) // LANE
    for count in range(1, SLOT // LANE + 1):
        pl.when(blocks == count)(functools.partial(body, count * LANE))


def fold(array):
    total = array[:, :LANE]
    for start in range(LANE, array.shape[1], LANE):
        total = total + array[:, start : start + LANE]
    return total


def live_row(length, columns):
    return (lax.broadcasted_iota(jnp.int32, (1, columns), 1) < length).astype(F32)


def mask_keys(scores, length):
    columns = scores.shape[0]
    start = columns - LANE
    last = scores[start:]
    key = lax.broadcasted_iota(jnp.int32, last.shape, 0) + start
    last = jnp.where(key < length, last, MASKED_SCORE)
    return last if start == 0 else jnp.concatenate([scores[:start], last], axis=0)


def normal(values):
    return 0.5 + 0.5 * lax.erf(values * 0.7071067811865476)


def colsum(array):
    return jnp.sum(array, axis=0, keepdims=True)


def rowsum(array):
    return jnp.sum(array, axis=1, keepdims=True)


def hold_kernel(lens, group, *refs):
    pass


def prepare_kernel(lens, group, rows, w_out, w_up, w_down, vec, bup, wo, wo_t, wup_t, wdown_t, flat):
    width = w_out.shape[0]
    flat[...] = jnp.transpose(w_out[...])
    for flip in range(GROUPS):
        block = flat[pl.ds(pl.multiple_of((group[0] ^ flip) * width, width), width), :]
        wo[flip] = jnp.transpose(block)
        if flip < 2:
            wo_t[flip] = block
    vectors = jnp.transpose(rows[...].astype(F32))
    vec[...] = vectors
    for part in range(bup.shape[0] // width):
        bup[part * width : (part + 1) * width, :] = vectors[:, 8 + part : 9 + part]
    wup_t[...] = jnp.transpose(w_up[...])
    wdown_t[...] = jnp.transpose(w_down[...])


def share_kernel(lens, group, shares, *rest):
    own = rest[-1]
    total = shares[0].astype(F32)
    for place in range(1, shares.shape[0]):
        total = total + shares[place].astype(F32)
    own[...] = jnp.broadcast_to(total.astype(BF16)[None], own.shape)


def turn_projection(wqkv, bias, wqkv_t, cols_qv):
    wqkv_t[...] = jnp.transpose(wqkv[...])
    cols_qv[...] = jnp.transpose(jnp.concatenate([bias[...].astype(F32)] * 4, axis=0))


def project(tokens, wqkv_t, cols_qv):
    width = tokens.shape[0]
    proj = nn(wqkv_t[...], tokens)
    query = ((proj[:width] + cols_qv[:, 0:1]) * SCALE).astype(BF16)
    key = proj[width : 2 * width].astype(BF16)
    value = (proj[2 * width :] + cols_qv[:, 1:2]).astype(BF16)
    return query, key, value


def attend_forward_kernel(
    first, count, lens, group, tok, wqkv, bias, w_out, ctx, lse, wqkv_t, cols_qv, flat
):
    step = pl.program_id(0)
    width = tok.shape[0]

    @pl.when(step == 0)
    def _():
        turn_projection(wqkv, bias, wqkv_t, cols_qv)

    @pl.when(step == count)
    def _():
        flat[...] = jnp.transpose(w_out[...])
        for place, flip in ((0, 2), (SLOT // 2, 3)):
            start = pl.multiple_of((group[0] ^ flip) * width, width)
            ctx[:, place : place + width] = flat[pl.ds(start, width), :]

    @pl.when(step < count)
    def _():
        attend_forward_step(
            lens[first + jnp.minimum(step, count - 1)], tok, ctx, lse, wqkv_t, cols_qv
        )


def attend_forward_step(length, tok, ctx, lse, wqkv_t, cols_qv):
    width = tok.shape[0]

    def body(columns):
        cols = slice(0, columns)
        query, key, value = project(tok[:, cols], wqkv_t, cols_qv)
        for head in range(width // HDIM):
            rows = slice(head * HDIM, (head + 1) * HDIM)
            scores = mask_keys(tn(key[rows], query[rows]), length)
            highest = jnp.max(scores, axis=0, keepdims=True)
            weights = jnp.exp(scores - highest)
            total = colsum(weights)
            ctx[rows, cols] = (nn(value[rows], weights.astype(BF16)) * (1.0 / total)).astype(BF16)
            lse[head : head + 1, cols] = highest + jnp.log(total)
        if columns < SLOT:
            ctx[:, columns:] = jnp.zeros((width, SLOT - columns), BF16)

    for_length(length, body)


def mix_kernel(
    first, lens, group, ctx0, ctx1, ctx2, ctx3, tok, wo0, wo1, wo2, wo3, vec, resid, stats
):
    length = lens[first + pl.program_id(0)]

    def body(columns):
        cols = slice(0, columns)
        total = tok[:, cols].astype(F32) + vec[:, 2:3]
        width = tok.shape[0]
        mixers = (
            wo0[...], wo1[...], wo2[:, :width], wo3[:, SLOT // 2 : SLOT // 2 + width]
        )
        for mixer, context in zip(mixers, (ctx0, ctx1, ctx2, ctx3)):
            total = total + nn(mixer, context[:, cols])
        resid[:, cols] = total
        stats[0:1, cols] = colsum(total)
        stats[1:2, cols] = colsum(total * total)

    for_length(length, body)


def first_norm(stats, cols):
    total = stats[0][:, cols] + stats[1][:, cols] + stats[2][:, cols]
    mean = total[0:1] / D
    inverse = lax.rsqrt(total[1:2] / D - mean * mean + EPSILON)
    return mean, inverse


def feed_forward_kernel(
    first, lens, group, resid, sa, sb, sc, cot, wup_t, wdown, vec, bup, hid, two, stats
):
    length = lens[first + pl.program_id(0)]

    def body(columns):
        cols = slice(0, columns)
        mean, inverse = first_norm((sa, sb, sc), cols)
        normed = (resid[:, cols] - mean) * inverse
        hidden = (normed * vec[:, 3:4] + vec[:, 4:5]).astype(BF16)
        hid[:, cols] = hidden
        pre_act = nn(wup_t[...], hidden) + bup[:, 0:1]
        activated = (pre_act * normal(pre_act)).astype(BF16)
        resid_two = hidden.astype(F32) + nn(wdown[...], activated) + vec[:, 5:6]
        two[:, cols] = resid_two
        grad = cot[:, cols].astype(F32) * live_row(length, columns) * vec[:, 6:7]
        stats[0:1, cols] = colsum(resid_two)
        stats[1:2, cols] = colsum(resid_two * resid_two)
        stats[2:3, cols] = colsum(grad)
        stats[3:4, cols] = colsum(grad * resid_two)

    for_length(length, body)


def feed_backward_kernel(
    first, has_earlier, lens, group, two, ta, tb, tc, cot, hid, resid, sa, sb, sc, wup_t, wdown_t,
    wup, vec, bup, *rest,
):
    *earlier, out, ghid, stats, grads, sums, sums_up = rest
    step = pl.program_id(0)
    length = lens[first + step]
    width, units = wup.shape

    @pl.when(step == 0)
    def _():
        grads[...] = earlier[0][...] if has_earlier else jnp.zeros_like(grads)
        sums[...] = jnp.zeros_like(sums)
        sums_up[...] = jnp.zeros_like(sums_up)

    def body(columns):
        cols = slice(0, columns)
        hidden = hid[:, cols]
        pre_act = nn(wup_t[...], hidden) + bup[:, 0:1]
        total = ta[:, cols] + tb[:, cols] + tc[:, cols]
        mean_two = total[0:1] / D
        inverse_two = lax.rsqrt(total[1:2] / D - mean_two * mean_two + EPSILON)
        normed_two = (two[:, cols] - mean_two) * inverse_two
        live = live_row(length, columns)
        out[:, cols] = ((normed_two * vec[:, 6:7] + vec[:, 7:8]) * live).astype(BF16)
        if columns < SLOT:
            out[:, columns:] = jnp.zeros((width, SLOT - columns), BF16)
        upstream = cot[:, cols].astype(F32) * live
        sums[0] += fold(upstream * normed_two)
        sums[1] += fold(upstream)
        plain = total[2:3] / D
        weighted = inverse_two * (total[3:4] - mean_two * total[2:3]) / D
        grad_two = (
            inverse_two * (upstream * vec[:, 6:7] - plain - normed_two * weighted)
        ).astype(BF16)
        grad_two_wide = grad_two.astype(F32)
        sums[2] += fold(grad_two_wide)
        grad_act = nn(wdown_t[...], grad_two)
        normal_cdf = normal(pre_act)
        activated = (pre_act * normal_cdf).astype(BF16)
        slope = normal_cdf + pre_act * (0.3989422804014327 * jnp.exp(-0.5 * pre_act * pre_act))
        grad_pre = (grad_act * slope).astype(BF16)
        sums_up[...] += fold(grad_pre.astype(F32))
        grad_hidden = (grad_two_wide + nn(wup[...], grad_pre)).astype(BF16)
        ghid[:, cols] = grad_hidden
        grads[:, :units] += nt(grad_two, activated)
        grads[:, units : 2 * units] += nt(hidden, grad_pre)
        grad_hidden = grad_hidden.astype(F32)
        mean, inverse = first_norm((sa, sb, sc), cols)
        normed = (resid[:, cols] - mean) * inverse
        sums[3] += fold(grad_hidden * normed)
        sums[4] += fold(grad_hidden)
        grad = grad_hidden * vec[:, 3:4]
        stats[0:1, cols] = colsum(grad)
        stats[1:2, cols] = colsum(grad * normed)

    for_length(length, body)

    @pl.when(step == pl.num_programs(0) - 1)
    def _():
        columns = [rowsum(sums[place]) for place in range(5)] + [jnp.zeros((width, 1), F32)]
        columns += [
            rowsum(sums_up[part * width : (part + 1) * width]) for part in range(units // width)
        ]
        for place, column in enumerate(columns):
            grads[:, 2 * units + place : 2 * units + place + 1] += column


def residual_grad_kernel(
    first, lens, group, ghid, ua, ub, uc, resid, sa, sb, sc, vec, *rest
):
    *_, gone, sums = rest
    length = lens[first + pl.program_id(0)]

    @pl.when(pl.program_id(0) == 0)
    def _():
        sums[...] = jnp.zeros_like(sums)

    def body(columns):
        cols = slice(0, columns)
        mean, inverse = first_norm((sa, sb, sc), cols)
        normed = (resid[:, cols] - mean) * inverse
        total = (ua[:, cols] + ub[:, cols] + uc[:, cols]) / D
        grad = ghid[:, cols].astype(F32) * vec[:, 3:4]
        grad_one = (inverse * (grad - total[0:1] - normed * total[1:2])).astype(BF16)
        gone[:, cols] = grad_one
        sums[...] += fold(grad_one.astype(F32))

    for_length(length, body)


def weight_grad_kernel(first, lens, group, gone, ctx0, ctx1, ctx2, ctx3, sums_out, *rest):
    *earlier, packed, dwo = rest
    step = pl.program_id(0)
    length = lens[first + step]
    width = gone.shape[0]

    @pl.when(step == 0)
    def _():
        dwo[...] = earlier[0][...] if earlier else jnp.zeros_like(dwo)

    def body(columns):
        cols = slice(0, columns)
        for place, context in enumerate((ctx0, ctx1, ctx2, ctx3)):
            dwo[place] += nt(context[:, cols], gone[:, cols])

    for_length(length, body)

    @pl.when(step == pl.num_programs(0) - 1)
    def _():
        if not earlier:
            packed[...] = dwo[...]
            return
        _, grads, sums_first = earlier
        double = grads.shape[1] - LANE
        start = double + GROUPS * width
        packed[:, :double] = grads[:, :double].astype(BF16)
        for place in range(GROUPS):
            packed[:, double + place * width : double + (place + 1) * width] = dwo[place].astype(BF16)
        lane = lax.broadcasted_iota(jnp.int32, (width, LANE), 1)
        bias = rowsum(sums_out[...]) + rowsum(sums_first[...])
        packed[:, start:] = jnp.where(lane == 5, bias, grads[:, double:]).astype(BF16)


def unpack_kernel(lens, group, packed, d0, d1, d2, d3, small, dwup, dwdown):
    width, units = dwup.shape
    dwdown[...] = packed[:, :units].astype(F32)
    dwup[...] = packed[:, units : 2 * units].astype(F32)
    for place, block in enumerate((d0, d1, d2, d3)):
        start = 2 * units + place * width
        block[...] = packed[:, start : start + width]
    small[...] = jnp.transpose(packed[:, 2 * units + GROUPS * width :].astype(F32))


def assemble_kernel(lens, group, d0, d1, d2, d3, out, blocks):
    width = d0.shape[0]
    for place, block in enumerate((d0, d1, d2, d3)):
        blocks[place] = block[...].astype(F32)
    for place in range(GROUPS):
        out[:, place * width : (place + 1) * width] = blocks[group[0] ^ place]


def unpack_qkv_kernel(lens, group, packed, bias, dwqkv):
    columns = dwqkv.shape[1]
    dwqkv[...] = packed[:, :columns].astype(F32)
    small = packed[:, columns:].astype(F32)
    bias[...] = jnp.transpose(jnp.concatenate([small, small], axis=1))[:2]


def attend_backward_kernel(
    first, has_earlier, lens, group, g0, g1, g2, g3, ctx, lse, tok, wo, wqkv, bias, *rest
):
    *earlier, gtok, packed, dwqkv, sums, gqkv, wqkv_t, cols_qv = rest
    step = pl.program_id(0)
    length = lens[first + step]
    width = tok.shape[0]

    @pl.when(step == 0)
    def _():
        if has_earlier:
            before = earlier[0]
            dwqkv[...] = before[:, : 3 * width]
        else:
            dwqkv[...] = jnp.zeros_like(dwqkv)
        sums[...] = jnp.zeros_like(sums)
        turn_projection(wqkv, bias, wqkv_t, cols_qv)

    def body(columns):
        cols = slice(0, columns)
        queries, keys, values = project(tok[:, cols], wqkv_t, cols_qv)
        grad_context = nn(wo[0], g0[:, cols])
        for place, grad in ((1, g1), (2, g2), (3, g3)):
            grad_context = grad_context + nn(wo[place], grad[:, cols])
        grad_context = grad_context.astype(BF16)
        shares = grad_context.astype(F32) * ctx[:, cols].astype(F32)
        inner = [
            colsum(shares[start : start + HDIM]) for start in range(0, width, HDIM)
        ]
        for head in range(width // HDIM):
            start = head * HDIM
            rows = slice(start, start + HDIM)
            query, key, value = queries[rows], keys[rows], values[rows]
            grad = grad_context[rows]
            scores = mask_keys(tn(key, query), length)
            probs = jnp.exp(scores - lse[head : head + 1, cols])
            grad_probs = tn(value, grad)
            grad_scores = (probs * (grad_probs - inner[head])).astype(BF16)
            gqkv[rows, cols] = (nn(key, grad_scores) * SCALE).astype(BF16)
            gqkv[width + start : width + start + HDIM, cols] = nt(query, grad_scores).astype(BF16)
            gqkv[2 * width + start : 2 * width + start + HDIM, cols] = nt(
                grad, probs.astype(BF16)
            ).astype(BF16)
        grad_proj = gqkv[:, cols]
        sums[0] += fold(grad_proj[:width].astype(F32))
        sums[1] += fold(grad_proj[2 * width :].astype(F32))
        dwqkv[...] += nt(tok[:, cols], grad_proj)
        gtok[:, cols] = (nn(wqkv[...], grad_proj) + g0[:, cols].astype(F32)).astype(BF16)
        if columns < SLOT:
            gtok[:, columns:] = jnp.zeros((width, SLOT - columns), BF16)

    for_length(length, body)

    @pl.when(step == pl.num_programs(0) - 1)
    def _():
        kind = packed.dtype
        tail = jnp.zeros((width, packed.shape[1] - 3 * width - 2), F32)
        small = jnp.concatenate([rowsum(sums[0]), rowsum(sums[1]), tail], axis=1)
        if has_earlier:
            small = small + earlier[0][:, 3 * width :]
        packed[:, : 3 * width] = dwqkv[...].astype(kind)
        packed[:, 3 * width :] = small.astype(kind)


def columns_of(rows, offset=0):
    return pl.BlockSpec((rows, SLOT), lambda i, lens, group: (0, i + offset))


def slots(rows):
    return pl.BlockSpec((None, rows, SLOT), lambda i, lens, group: (i, 0, 0))


def slot_at(place, rows):
    return pl.BlockSpec((None, rows, SLOT), lambda i, lens, group: (place, 0, 0))


def group_slots(rows, flip, count):
    return pl.BlockSpec(
        (None, rows, SLOT), lambda i, lens, group: ((group[0] ^ flip) * count + i, 0, 0)
    )


def whole(*shape):
    return pl.BlockSpec(shape, lambda i, lens, group: (0,) * len(shape))


def call(chain, kernel, name, count, scalars, ins, outs, scratch=(), aliases=None, us=0.0, vmem=None):
    body, after = kernel, list(chain)
    if after:
        place = len(scalars) + len(ins)
        ins = ins + [(array, pl.BlockSpec(memory_space=pl.ANY)) for array in after]

        def body(*refs):
            return kernel(*refs[:place], *refs[place + len(after) :])

    results = pl.pallas_call(
        body,
        out_shape=[jax.ShapeDtypeStruct(shape, kind) for shape, kind, _ in outs],
        grid_spec=pltpu.PrefetchScalarGridSpec(
            num_scalar_prefetch=len(scalars),
            grid=(count,),
            in_specs=[block for _, block in ins],
            out_specs=[block for _, _, block in outs],
            scratch_shapes=list(scratch),
        ),
        input_output_aliases=aliases or {},
        compiler_params=pltpu.CompilerParams(
            dimension_semantics=("arbitrary",), vmem_limit_bytes=(vmem or MID_VMEM) * 2**20
        ),
        cost_estimate=pl.CostEstimate(
            flops=int(us * COST * 1.1e9), bytes_accessed=0, transcendentals=0
        ),
        name=name,
    )(*scalars, *[array for array, _ in ins])
    chain[:] = [results[-1]]
    return results


def permute(array, flip):
    return lax.ppermute(array, "grp", [(g, g ^ flip) for g in range(GROUPS)])


def send_wide(array, way):
    if way == "gather":
        return [array, lax.all_gather(array, "grp", axis=0, tiled=True)]
    return [array, permute(array, 1), permute(array, 2)]


def spread_wide(array, *others):
    count, rows, _ = array.shape
    if len(others) == 1:
        return [(array, slots(rows))] + [
            (others[0], group_slots(rows, flip, count)) for flip in (1, 2, 3)
        ]
    near, across = others
    return [(a, slots(rows)) for a in (array, near, across, permute(across, 1))]


def gather_small(array):
    near = permute(array, 1)
    return [(a, slots(array.shape[1])) for a in (array, near, permute(array + near, 2))]


def scatter_over_seq(packed):
    ranks = lax.axis_size("seq")
    rows, columns = packed.shape
    return lax.all_to_all(packed.reshape(ranks, rows // ranks, columns), "seq", 0, 0)


def sum_over_seq(chain, scalars, shares, held=()):
    ranks, rows, columns = shares.shape
    block = whole(ranks, rows, columns)
    place = pl.BlockSpec(memory_space=pl.ANY)
    *passed, own = call(
        chain, share_kernel, "share", 1, scalars, [(shares, block)] + [(h, place) for h in held],
        [(h.shape, h.dtype, place) for h in held] + [(shares.shape, BF16, block)],
        aliases={len(scalars) + 1 + n: n for n in range(len(held))}, us=1.0,
    )
    return lax.all_to_all(own, "seq", 0, 0).reshape(ranks * rows, columns), passed


def hold(chain, scalars, arrays):
    place = pl.BlockSpec(memory_space=pl.ANY)
    return call(
        chain, hold_kernel, "hold", 1, scalars, [(a, place) for a in arrays],
        [(a.shape, a.dtype, place) for a in arrays],
        aliases={len(scalars) + n: n for n in range(len(arrays))},
    )


def local(
    tokens, lengths, w_qkv, b_qv, w_out, b_out, ln1_gain, ln1_bias, w_up, b_up, w_down, b_down,
    ln2_gain, ln2_bias, cotangent,
):
    width, row_count = tokens.shape
    units = w_up.shape[1]
    seq_count = lengths.shape[0]
    group = lax.axis_index("grp").astype(jnp.int32)
    scalars = (lengths, group[None])
    parts = units // width
    rows = jnp.concatenate(
        [b_qv.reshape(-1), b_out, ln1_gain, ln1_bias, b_down, ln2_gain, ln2_bias, b_up]
    ).reshape(8 + parts, width)
    chain = []
    middle = int(seq_count * FIRST_CHUNK)
    chunks = [(0, middle), (middle, seq_count - middle)]
    untouched = pl.BlockSpec(memory_space=pl.ANY)
    state = [{}, {}]
    shared = dict(output=None, grad_tokens=None, packed=None, packed_qkv=None)
    pack_width = 2 * units + GROUPS * width + LANE
    qkv_width = 3 * width + LANE // 2
    square = ((width, width), BF16, whole(width, width))

    def prepare(_):
        turned = ((units, width), BF16, whole(units, width))
        shared["vec"], shared["bup"], shared["wo"], wo_t, shared["wup_t"], shared["wdown_t"] = call(
            chain, prepare_kernel, "prepare", 1, scalars,
            [
                (rows, whole(8 + parts, width)), (w_out, whole(width, D)),
                (w_up, whole(width, units)), (w_down, whole(width, units)),
            ],
            [
                ((width, 8 + parts), F32, whole(width, 8 + parts)),
                ((units, 1), F32, whole(units, 1)),
                ((GROUPS, width, width), BF16, whole(GROUPS, width, width)),
                ((2, width, width), BF16, whole(2, width, width)), turned, turned,
            ],
            scratch=[pltpu.VMEM((D, width), BF16)], vmem=VMEM,
        )
        shared["mixers"] = [
            (wo_t, pl.BlockSpec((None, width, width), lambda i, lens, group: (0, 0, 0))),
            (permute(wo_t[1], 1), whole(width, width)),
        ]

    def attend(which):
        first, count = chunks[which]
        steps = count + 1 if which == 0 else count
        near_end = lambda i, lens, group: (0, first + jnp.minimum(i, count - 1))
        held = lambda height: pl.BlockSpec(
            (None, height, SLOT), lambda i, lens, group: (jnp.minimum(i, count - 1), 0, 0)
        )
        context, lse = call(
            chain, functools.partial(attend_forward_kernel, first, count), "attend_forward", steps,
            scalars,
            [
                (tokens, pl.BlockSpec((width, SLOT), near_end)), (w_qkv, whole(width, 3 * width)),
                (b_qv, whole(2, width)), (w_out, whole(width, D)),
            ],
            [
                ((steps, width, SLOT), BF16, slots(width)),
                ((count, 8, SLOT), F32, held(8)),
            ],
            scratch=[
                pltpu.VMEM((3 * width, width), BF16), pltpu.VMEM((width, 8), F32),
                pltpu.VMEM((D, width), BF16),
            ],
            us=ATTEND_US, vmem=ATTEND_VMEM[which],
        )
        state[which].update(context=send_wide(context, CONTEXT_WAYS[which]), lse=lse)

    def hold_context(which):
        mine = state[which]
        if CONTEXT_WAYS[which] == "permute" and which in CONTEXT_HELD:
            mine["context"][2:] = hold(chain, scalars, mine["context"][2:])
        mine["contexts"] = spread_wide(*mine["context"])
        if which == 0:
            place = chunks[0][1]
            shared["mixers"] += [
                (array, slot_at(place, width)) for array, _ in mine["contexts"][2:]
            ]

    def mix(which):
        (first, count), mine = chunks[which], state[which]
        mine["resid"], stats = call(
            chain, functools.partial(mix_kernel, first), "mix", count, scalars,
            mine["contexts"] + [(tokens, columns_of(width, first))] + shared["mixers"]
            + [(shared["vec"], whole(width, 8 + parts))],
            [((count, width, SLOT), F32, slots(width)), ((count, 2, SLOT), F32, slots(2))],
            us=3.0 * MIDDLE_US,
        )
        mine["one"] = gather_small(stats)

    def feed_forward(which):
        (first, count), mine = chunks[which], state[which]
        mine["hid"], mine["two"], stats = call(
            chain, functools.partial(feed_forward_kernel, first), "feed_forward", count, scalars,
            [(mine["resid"], slots(width))] + mine["one"] + [
                (cotangent, columns_of(width, first)), (shared["wup_t"], whole(units, width)),
                (w_down, whole(width, units)), (shared["vec"], whole(width, 8 + parts)),
                (shared["bup"], whole(units, 1)),
            ],
            [
                ((count, width, SLOT), BF16, slots(width)),
                ((count, width, SLOT), F32, slots(width)),
                ((count, 4, SLOT), F32, slots(4)),
            ],
            us=8.0 * MIDDLE_US,
        )
        mine["second"] = gather_small(stats)

    def feed_backward(which):
        (first, count), mine = chunks[which], state[which]
        grads = ((width, 2 * units + LANE), F32, whole(width, 2 * units + LANE))
        ins = [(mine["two"], slots(width))] + mine["second"] + [
            (cotangent, columns_of(width, first)), (mine["hid"], slots(width)),
            (mine["resid"], slots(width)),
        ] + mine["one"] + [
            (shared["wup_t"], whole(units, width)), (shared["wdown_t"], whole(units, width)),
            (w_up, whole(width, units)), (shared["vec"], whole(width, 8 + parts)),
            (shared["bup"], whole(units, 1)),
        ]
        aliases, has_earlier = {}, shared["output"] is not None
        if has_earlier:
            ins.append((shared["grads"], grads[2]))
            aliases = {len(scalars) + len(ins): 0}
            ins.append((shared["output"], untouched))
        shared["output"], mine["ghid"], stats, shared["grads"] = call(
            chain, functools.partial(feed_backward_kernel, first, has_earlier), "feed_backward",
            count, scalars, ins,
            [
                ((width, row_count), BF16, columns_of(width, first)),
                ((count, width, SLOT), BF16, slots(width)),
                ((count, 2, SLOT), F32, slots(2)), grads,
            ],
            scratch=[pltpu.VMEM((5, width, LANE), F32), pltpu.VMEM((units, LANE), F32)],
            aliases=aliases, us=8.0 * MIDDLE_US,
        )
        mine["third"] = gather_small(stats)

    def wait_third(_):
        chain.extend(state[which]["third"][2][0] for which in (0, 1))

    def residual_grad(which):
        (first, count), mine = chunks[which], state[which]
        gone, mine["out"] = call(
            chain, functools.partial(residual_grad_kernel, first), "residual_grad", count, scalars,
            [(mine["ghid"], slots(width))] + mine["third"] + [(mine["resid"], slots(width))]
            + mine["one"] + [(shared["vec"], whole(width, 8 + parts))],
            [((count, width, SLOT), BF16, slots(width)), ((width, LANE), F32, whole(width, LANE))],
            us=2.0 * MIDDLE_US,
        )
        mine["gone"] = send_wide(gone, GRADIENT_WAYS[which])

    def weight_grad(which):
        (first, count), mine = chunks[which], state[which]
        final = shared["packed"] is not None
        ins = [
            (mine["gone"][0], slots(width)), *mine["contexts"], (mine["out"], whole(width, LANE)),
        ]
        result = ((GROUPS, width, width), F32, whole(GROUPS, width, width))
        if final:
            ins += [
                (shared["packed"], result[2]),
                (shared["grads"], whole(width, 2 * units + LANE)),
                (state[1 - which]["out"], whole(width, LANE)),
            ]
            result = ((width, pack_width), BF16, whole(width, pack_width))
        (shared["packed"],) = call(
            chain, functools.partial(weight_grad_kernel, first), "weight_grad", count, scalars, ins,
            [result], scratch=[pltpu.VMEM((GROUPS, width, width), F32)], us=WEIGHT_US[final],
        )
        if final:
            shared["shares"] = scatter_over_seq(shared["packed"])

    def share(which):
        mine = state[which]
        shared["weight_sums"], far = sum_over_seq(
            chain, scalars, shared["shares"], mine["gone"][2:] if which in GRADIENT_HELD else ()
        )
        if far:
            mine["gone"][2:] = far

    def hold_gone(which):
        mine = state[which]
        mine["gone"][2:] = hold(chain, scalars, mine["gone"][2:])

    def attend_backward(which):
        (first, count), mine = chunks[which], state[which]
        final = shared["packed_qkv"] is not None
        ins = [
            *spread_wide(*mine["gone"]), (mine["contexts"][0][0], slots(width)),
            (mine["lse"], slots(8)),
            (tokens, columns_of(width, first)), (shared["wo"], whole(GROUPS, width, width)),
            (w_qkv, whole(width, 3 * width)), (b_qv, whole(2, width)),
        ]
        aliases = {}
        if final:
            ins.append((shared["packed_qkv"], whole(width, qkv_width)))
            aliases = {len(scalars) + len(ins): 0}
            ins.append((shared["grad_tokens"], untouched))
        shared["grad_tokens"], shared["packed_qkv"] = call(
            chain, functools.partial(attend_backward_kernel, first, final), "attend_backward", count,
            scalars, ins,
            [
                ((width, row_count), BF16, columns_of(width, first)),
                ((width, qkv_width), BF16 if final else F32, whole(width, qkv_width)),
            ],
            scratch=[
                pltpu.VMEM((width, 3 * width), F32), pltpu.VMEM((2, width, LANE), F32),
                pltpu.VMEM((3 * width, SLOT), BF16),
                pltpu.VMEM((3 * width, width), BF16), pltpu.VMEM((width, 8), F32),
            ],
            aliases=aliases, us=BACKWARD_US[final], vmem=BACKWARD_VMEM[final],
        )

    stages = dict(
        P=prepare, A=attend, H=hold_context, M=mix, U=feed_forward, B=feed_backward, R=residual_grad,
        T=wait_third, W=weight_grad, S=share, G=hold_gone, D=attend_backward,
    )
    for stage in ORDER:
        stages[stage[0]](int(stage[1]))
    output, grad_tokens = shared["output"], shared["grad_tokens"]
    shares_qkv = scatter_over_seq(shared["packed_qkv"])
    *blocks, small, grad_w_up, grad_w_down = call(
        chain, unpack_kernel, "unpack", 1, scalars,
        [(shared["weight_sums"], whole(width, pack_width))],
        [
            square, square, square, square,
            ((LANE, width), F32, whole(LANE, width)),
            ((width, units), F32, whole(width, units)),
            ((width, units), F32, whole(width, units)),
        ],
        us=3.0,
    )
    qkv_sums, _ = sum_over_seq(chain, scalars, shares_qkv)
    routed = [blocks[0]] + [permute(blocks[flip], flip) for flip in (1, 2, 3)]
    (grad_w_out,) = call(
        chain, assemble_kernel, "assemble", 1, scalars,
        [(block, whole(width, width)) for block in routed],
        [((width, D), F32, whole(width, D))],
        scratch=[pltpu.VMEM((GROUPS, width, width), F32)], us=1.0,
    )
    grad_b_qv, grad_w_qkv = call(
        chain, unpack_qkv_kernel, "unpack_qkv", 1, scalars, [(qkv_sums, whole(width, qkv_width))],
        [((2, width), F32, whole(2, width)), ((width, 3 * width), F32, whole(width, 3 * width))],
    )
    return (
        output, grad_tokens, grad_w_qkv, grad_b_qv, grad_w_out, small[5], small[3], small[4],
        grad_w_up, small[6 : 6 + parts].reshape(-1), grad_w_down, small[2], small[0], small[1],
    )


def solution(mesh):
    row, vector = P("grp", None), P("grp")
    placed = (
        P("grp", "seq"), P("seq"), row, P(None, "grp"), row, vector, vector, vector, row, vector,
        row, vector, vector, vector, P("grp", "seq"),
    )
    results = (
        P("grp", "seq"), P("grp", "seq"), row, P(None, "grp"), row, vector, vector, vector, row,
        vector, row, vector, vector, vector,
    )
    return jax.shard_map(local, mesh=mesh, in_specs=placed, out_specs=results, check_vma=False)
```

```python
import functools
import math

import jax
import jax.numpy as jnp
from jax import lax
from jax.experimental import pallas as pl
from jax.experimental.pallas import tpu as pltpu
from jax.sharding import PartitionSpec as P

D = 768
HDIM = 64
SLOT = 512
LANE = 128
GROUPS = 4
EPSILON = 1e-06
MASKED_SCORE = -1000000000.0
SCALE = 1.0 / math.sqrt(HDIM)
FIRST_CHUNK = 0.5
ORDER = ("A0", "P0", "A1", "H0", "M0", "H1", "M1", "U0", "U1", "B0", "B1", "T0", "R0", "R1", "W0", "W1", "G0", "D0", "S1", "G1", "D1")
WEIGHT_US = 8.0, 8.0
BACKWARD_US = 4.0, 20.0
ATTEND_US = 8.0
MIDDLE_US = 1.0
CONTEXT_WAYS = "permute", "permute"
CONTEXT_HELD = ()
GRADIENT_WAYS = "permute", "permute"
GRADIENT_HELD = ()
VMEM = 60
ATTEND_VMEM = 60, 20
BACKWARD_VMEM = 20, 20
MID_VMEM = 16
COST = 1.0
F32 = jnp.float32
BF16 = jnp.bfloat16


def nn(left, right):
    return lax.dot_general(left, right, (((1,), (0,)), ((), ())), preferred_element_type=F32)


def tn(left, right):
    return lax.dot_general(left, right, (((0,), (0,)), ((), ())), preferred_element_type=F32)


def nt(left, right):
    return lax.dot_general(left, right, (((1,), (1,)), ((), ())), preferred_element_type=F32)


def for_length(length, body):
    blocks = (length + (LANE - 1)) // LANE
    for count in range(1, SLOT // LANE + 1):
        pl.when(blocks == count)(functools.partial(body, count * LANE))


def fold(array):
    total = array[:, :LANE]
    for start in range(LANE, array.shape[1], LANE):
        total = total + array[:, start : start + LANE]
    return total


def live_row(length, columns):
    return (lax.broadcasted_iota(jnp.int32, (1, columns), 1) < length).astype(F32)


def mask_keys(scores, length):
    columns = scores.shape[0]
    start = columns - LANE
    last = scores[start:]
    key = lax.broadcasted_iota(jnp.int32, last.shape, 0) + start
    last = jnp.where(key < length, last, MASKED_SCORE)
    return last if start == 0 else jnp.concatenate([scores[:start], last], axis=0)


def normal(values):
    return 0.5 + 0.5 * lax.erf(values * 0.7071067811865476)


def colsum(array):
    return jnp.sum(array, axis=0, keepdims=True)


def rowsum(array):
    return jnp.sum(array, axis=1, keepdims=True)


def hold_kernel(lens, group, *refs):
    pass


def prepare_kernel(lens, group, rows, w_out, w_up, w_down, vec, bup, wo, wo_t, wup_t, wdown_t, flat):
    width = w_out.shape[0]
    flat[...] = jnp.transpose(w_out[...])
    for flip in range(GROUPS):
        block = flat[pl.ds(pl.multiple_of((group[0] ^ flip) * width, width), width), :]
        wo[flip] = jnp.transpose(block)
        if flip < 2:
            wo_t[flip] = block
    vectors = jnp.transpose(rows[...].astype(F32))
    vec[...] = vectors
    for part in range(bup.shape[0] // width):
        bup[part * width : (part + 1) * width, :] = vectors[:, 8 + part : 9 + part]
    wup_t[...] = jnp.transpose(w_up[...])
    wdown_t[...] = jnp.transpose(w_down[...])


def share_kernel(lens, group, shares, *rest):
    own = rest[-1]
    total = shares[0].astype(F32)
    for place in range(1, shares.shape[0]):
        total = total + shares[place].astype(F32)
    own[...] = jnp.broadcast_to(total.astype(BF16)[None], own.shape)


def turn_projection(wqkv, bias, wqkv_t, cols_qv):
    wqkv_t[...] = jnp.transpose(wqkv[...])
    cols_qv[...] = jnp.transpose(jnp.concatenate([bias[...].astype(F32)] * 4, axis=0))


def project(tokens, wqkv_t, cols_qv):
    width = tokens.shape[0]
    proj = nn(wqkv_t[...], tokens)
    query = ((proj[:width] + cols_qv[:, 0:1]) * SCALE).astype(BF16)
    key = proj[width : 2 * width].astype(BF16)
    value = (proj[2 * width :] + cols_qv[:, 1:2]).astype(BF16)
    return query, key, value


def attend_forward_kernel(
    first, count, lens, group, tok, wqkv, bias, w_out, ctx, lse, wqkv_t, cols_qv, flat
):
    step = pl.program_id(0)
    width = tok.shape[0]

    @pl.when(step == 0)
    def _():
        turn_projection(wqkv, bias, wqkv_t, cols_qv)

    @pl.when(step == count)
    def _():
        flat[...] = jnp.transpose(w_out[...])
        for place, flip in ((0, 2), (SLOT // 2, 3)):
            start = pl.multiple_of((group[0] ^ flip) * width, width)
            ctx[:, place : place + width] = flat[pl.ds(start, width), :]

    @pl.when(step < count)
    def _():
        attend_forward_step(
            lens[first + jnp.minimum(step, count - 1)], tok, ctx, lse, wqkv_t, cols_qv
        )


def attend_forward_step(length, tok, ctx, lse, wqkv_t, cols_qv):
    width = tok.shape[0]

    def body(columns):
        cols = slice(0, columns)
        query, key, value = project(tok[:, cols], wqkv_t, cols_qv)
        for head in range(width // HDIM):
            rows = slice(head * HDIM, (head + 1) * HDIM)
            scores = mask_keys(tn(key[rows], query[rows]), length)
            highest = jnp.max(scores, axis=0, keepdims=True)
            weights = jnp.exp(scores - highest)
            total = colsum(weights)
            ctx[rows, cols] = (nn(value[rows], weights.astype(BF16)) * (1.0 / total)).astype(BF16)
            lse[head : head + 1, cols] = highest + jnp.log(total)
        if columns < SLOT:
            ctx[:, columns:] = jnp.zeros((width, SLOT - columns), BF16)

    for_length(length, body)


def mix_kernel(
    first, lens, group, ctx0, ctx1, ctx2, ctx3, tok, wo0, wo1, wo2, wo3, vec, resid, stats
):
    length = lens[first + pl.program_id(0)]

    def body(columns):
        cols = slice(0, columns)
        total = tok[:, cols].astype(F32) + vec[:, 2:3]
        width = tok.shape[0]
        mixers = (
            wo0[...], wo1[...], wo2[:, :width], wo3[:, SLOT // 2 : SLOT // 2 + width]
        )
        for mixer, context in zip(mixers, (ctx0, ctx1, ctx2, ctx3)):
            total = total + nn(mixer, context[:, cols])
        resid[:, cols] = total
        stats[0:1, cols] = colsum(total)
        stats[1:2, cols] = colsum(total * total)

    for_length(length, body)


def first_norm(stats, cols):
    total = stats[0][:, cols] + stats[1][:, cols] + stats[2][:, cols]
    mean = total[0:1] / D
    inverse = lax.rsqrt(total[1:2] / D - mean * mean + EPSILON)
    return mean, inverse


def feed_forward_kernel(
    first, lens, group, resid, sa, sb, sc, cot, wup_t, wdown, vec, bup, hid, two, stats
):
    length = lens[first + pl.program_id(0)]

    def body(columns):
        cols = slice(0, columns)
        mean, inverse = first_norm((sa, sb, sc), cols)
        normed = (resid[:, cols] - mean) * inverse
        hidden = (normed * vec[:, 3:4] + vec[:, 4:5]).astype(BF16)
        hid[:, cols] = hidden
        pre_act = nn(wup_t[...], hidden) + bup[:, 0:1]
        activated = (pre_act * normal(pre_act)).astype(BF16)
        resid_two = hidden.astype(F32) + nn(wdown[...], activated) + vec[:, 5:6]
        two[:, cols] = resid_two
        grad = cot[:, cols].astype(F32) * live_row(length, columns) * vec[:, 6:7]
        stats[0:1, cols] = colsum(resid_two)
        stats[1:2, cols] = colsum(resid_two * resid_two)
        stats[2:3, cols] = colsum(grad)
        stats[3:4, cols] = colsum(grad * resid_two)

    for_length(length, body)


def feed_backward_kernel(
    first, has_earlier, lens, group, two, ta, tb, tc, cot, hid, resid, sa, sb, sc, wup_t, wdown_t,
    wup, vec, bup, *rest,
):
    *earlier, out, ghid, stats, grads, sums, sums_up = rest
    step = pl.program_id(0)
    length = lens[first + step]
    width, units = wup.shape

    @pl.when(step == 0)
    def _():
        grads[...] = earlier[0][...] if has_earlier else jnp.zeros_like(grads)
        sums[...] = jnp.zeros_like(sums)
        sums_up[...] = jnp.zeros_like(sums_up)

    def body(columns):
        cols = slice(0, columns)
        hidden = hid[:, cols]
        pre_act = nn(wup_t[...], hidden) + bup[:, 0:1]
        total = ta[:, cols] + tb[:, cols] + tc[:, cols]
        mean_two = total[0:1] / D
        inverse_two = lax.rsqrt(total[1:2] / D - mean_two * mean_two + EPSILON)
        normed_two = (two[:, cols] - mean_two) * inverse_two
        live = live_row(length, columns)
        out[:, cols] = ((normed_two * vec[:, 6:7] + vec[:, 7:8]) * live).astype(BF16)
        if columns < SLOT:
            out[:, columns:] = jnp.zeros((width, SLOT - columns), BF16)
        upstream = cot[:, cols].astype(F32) * live
        sums[0] += fold(upstream * normed_two)
        sums[1] += fold(upstream)
        plain = total[2:3] / D
        weighted = inverse_two * (total[3:4] - mean_two * total[2:3]) / D
        grad_two = (
            inverse_two * (upstream * vec[:, 6:7] - plain - normed_two * weighted)
        ).astype(BF16)
        grad_two_wide = grad_two.astype(F32)
        sums[2] += fold(grad_two_wide)
        grad_act = nn(wdown_t[...], grad_two)
        normal_cdf = normal(pre_act)
        activated = (pre_act * normal_cdf).astype(BF16)
        slope = normal_cdf + pre_act * (0.3989422804014327 * jnp.exp(-0.5 * pre_act * pre_act))
        grad_pre = (grad_act * slope).astype(BF16)
        sums_up[...] += fold(grad_pre.astype(F32))
        grad_hidden = (grad_two_wide + nn(wup[...], grad_pre)).astype(BF16)
        ghid[:, cols] = grad_hidden
        grads[:, :units] += nt(grad_two, activated)
        grads[:, units : 2 * units] += nt(hidden, grad_pre)
        grad_hidden = grad_hidden.astype(F32)
        mean, inverse = first_norm((sa, sb, sc), cols)
        normed = (resid[:, cols] - mean) * inverse
        sums[3] += fold(grad_hidden * normed)
        sums[4] += fold(grad_hidden)
        grad = grad_hidden * vec[:, 3:4]
        stats[0:1, cols] = colsum(grad)
        stats[1:2, cols] = colsum(grad * normed)

    for_length(length, body)

    @pl.when(step == pl.num_programs(0) - 1)
    def _():
        columns = [rowsum(sums[place]) for place in range(5)] + [jnp.zeros((width, 1), F32)]
        columns += [
            rowsum(sums_up[part * width : (part + 1) * width]) for part in range(units // width)
        ]
        for place, column in enumerate(columns):
            grads[:, 2 * units + place : 2 * units + place + 1] += column


def residual_grad_kernel(
    first, lens, group, ghid, ua, ub, uc, resid, sa, sb, sc, vec, *rest
):
    *_, gone, sums = rest
    length = lens[first + pl.program_id(0)]

    @pl.when(pl.program_id(0) == 0)
    def _():
        sums[...] = jnp.zeros_like(sums)

    def body(columns):
        cols = slice(0, columns)
        mean, inverse = first_norm((sa, sb, sc), cols)
        normed = (resid[:, cols] - mean) * inverse
        total = (ua[:, cols] + ub[:, cols] + uc[:, cols]) / D
        grad = ghid[:, cols].astype(F32) * vec[:, 3:4]
        grad_one = (inverse * (grad - total[0:1] - normed * total[1:2])).astype(BF16)
        gone[:, cols] = grad_one
        sums[...] += fold(grad_one.astype(F32))

    for_length(length, body)


def weight_grad_kernel(first, lens, group, gone, ctx0, ctx1, ctx2, ctx3, sums_out, *rest):
    *earlier, packed, dwo = rest
    step = pl.program_id(0)
    length = lens[first + step]
    width = gone.shape[0]

    @pl.when(step == 0)
    def _():
        dwo[...] = earlier[0][...] if earlier else jnp.zeros_like(dwo)

    def body(columns):
        cols = slice(0, columns)
        for place, context in enumerate((ctx0, ctx1, ctx2, ctx3)):
            dwo[place] += nt(context[:, cols], gone[:, cols])

    for_length(length, body)

    @pl.when(step == pl.num_programs(0) - 1)
    def _():
        if not earlier:
            packed[...] = dwo[...]
            return
        _, grads, sums_first = earlier
        double = grads.shape[1] - LANE
        start = double + GROUPS * width
        packed[:, :double] = grads[:, :double].astype(BF16)
        for place in range(GROUPS):
            packed[:, double + place * width : double + (place + 1) * width] = dwo[place].astype(BF16)
        lane = lax.broadcasted_iota(jnp.int32, (width, LANE), 1)
        bias = rowsum(sums_out[...]) + rowsum(sums_first[...])
        packed[:, start:] = jnp.where(lane == 5, bias, grads[:, double:]).astype(BF16)


def unpack_kernel(lens, group, packed, d0, d1, d2, d3, small, dwup, dwdown):
    width, units = dwup.shape
    dwdown[...] = packed[:, :units].astype(F32)
    dwup[...] = packed[:, units : 2 * units].astype(F32)
    for place, block in enumerate((d0, d1, d2, d3)):
        start = 2 * units + place * width
        block[...] = packed[:, start : start + width]
    small[...] = jnp.transpose(packed[:, 2 * units + GROUPS * width :].astype(F32))


def assemble_kernel(lens, group, d0, d1, d2, d3, out, blocks):
    width = d0.shape[0]
    for place, block in enumerate((d0, d1, d2, d3)):
        blocks[place] = block[...].astype(F32)
    for place in range(GROUPS):
        out[:, place * width : (place + 1) * width] = blocks[group[0] ^ place]


def unpack_qkv_kernel(lens, group, packed, bias, dwqkv):
    columns = dwqkv.shape[1]
    dwqkv[...] = packed[:, :columns].astype(F32)
    small = packed[:, columns:].astype(F32)
    bias[...] = jnp.transpose(jnp.concatenate([small, small], axis=1))[:2]


def attend_backward_kernel(
    first, has_earlier, lens, group, g0, g1, g2, g3, ctx, lse, tok, wo, wqkv, bias, *rest
):
    *earlier, gtok, packed, dwqkv, sums, gqkv, wqkv_t, cols_qv = rest
    step = pl.program_id(0)
    length = lens[first + step]
    width = tok.shape[0]

    @pl.when(step == 0)
    def _():
        if has_earlier:
            before = earlier[0]
            dwqkv[...] = before[:, : 3 * width]
        else:
            dwqkv[...] = jnp.zeros_like(dwqkv)
        sums[...] = jnp.zeros_like(sums)
        turn_projection(wqkv, bias, wqkv_t, cols_qv)

    def body(columns):
        cols = slice(0, columns)
        queries, keys, values = project(tok[:, cols], wqkv_t, cols_qv)
        grad_context = nn(wo[0], g0[:, cols])
        for place, grad in ((1, g1), (2, g2), (3, g3)):
            grad_context = grad_context + nn(wo[place], grad[:, cols])
        grad_context = grad_context.astype(BF16)
        shares = grad_context.astype(F32) * ctx[:, cols].astype(F32)
        inner = [
            colsum(shares[start : start + HDIM]) for start in range(0, width, HDIM)
        ]
        for head in range(width // HDIM):
            start = head * HDIM
            rows = slice(start, start + HDIM)
            query, key, value = queries[rows], keys[rows], values[rows]
            grad = grad_context[rows]
            scores = mask_keys(tn(key, query), length)
            probs = jnp.exp(scores - lse[head : head + 1, cols])
            grad_probs = tn(value, grad)
            grad_scores = (probs * (grad_probs - inner[head])).astype(BF16)
            gqkv[rows, cols] = (nn(key, grad_scores) * SCALE).astype(BF16)
            gqkv[width + start : width + start + HDIM, cols] = nt(query, grad_scores).astype(BF16)
            gqkv[2 * width + start : 2 * width + start + HDIM, cols] = nt(
                grad, probs.astype(BF16)
            ).astype(BF16)
        grad_proj = gqkv[:, cols]
        sums[0] += fold(grad_proj[:width].astype(F32))
        sums[1] += fold(grad_proj[2 * width :].astype(F32))
        dwqkv[...] += nt(tok[:, cols], grad_proj)
        gtok[:, cols] = (nn(wqkv[...], grad_proj) + g0[:, cols].astype(F32)).astype(BF16)
        if columns < SLOT:
            gtok[:, columns:] = jnp.zeros((width, SLOT - columns), BF16)

    for_length(length, body)

    @pl.when(step == pl.num_programs(0) - 1)
    def _():
        kind = packed.dtype
        tail = jnp.zeros((width, packed.shape[1] - 3 * width - 2), F32)
        small = jnp.concatenate([rowsum(sums[0]), rowsum(sums[1]), tail], axis=1)
        if has_earlier:
            small = small + earlier[0][:, 3 * width :]
        packed[:, : 3 * width] = dwqkv[...].astype(kind)
        packed[:, 3 * width :] = small.astype(kind)


def columns_of(rows, offset=0):
    return pl.BlockSpec((rows, SLOT), lambda i, lens, group: (0, i + offset))


def slots(rows):
    return pl.BlockSpec((None, rows, SLOT), lambda i, lens, group: (i, 0, 0))


def slot_at(place, rows):
    return pl.BlockSpec((None, rows, SLOT), lambda i, lens, group: (place, 0, 0))


def group_slots(rows, flip, count):
    return pl.BlockSpec(
        (None, rows, SLOT), lambda i, lens, group: ((group[0] ^ flip) * count + i, 0, 0)
    )


def whole(*shape):
    return pl.BlockSpec(shape, lambda i, lens, group: (0,) * len(shape))


def call(chain, kernel, name, count, scalars, ins, outs, scratch=(), aliases=None, us=0.0, vmem=None):
    body, after = kernel, list(chain)
    if after:
        place = len(scalars) + len(ins)
        ins = ins + [(array, pl.BlockSpec(memory_space=pl.ANY)) for array in after]

        def body(*refs):
            return kernel(*refs[:place], *refs[place + len(after) :])

    results = pl.pallas_call(
        body,
        out_shape=[jax.ShapeDtypeStruct(shape, kind) for shape, kind, _ in outs],
        grid_spec=pltpu.PrefetchScalarGridSpec(
            num_scalar_prefetch=len(scalars),
            grid=(count,),
            in_specs=[block for _, block in ins],
            out_specs=[block for _, _, block in outs],
            scratch_shapes=list(scratch),
        ),
        input_output_aliases=aliases or {},
        compiler_params=pltpu.CompilerParams(
            dimension_semantics=("arbitrary",), vmem_limit_bytes=(vmem or MID_VMEM) * 2**20
        ),
        cost_estimate=pl.CostEstimate(
            flops=int(us * COST * 1.1e9), bytes_accessed=0, transcendentals=0
        ),
        name=name,
    )(*scalars, *[array for array, _ in ins])
    chain[:] = [results[-1]]
    return results


def permute(array, flip):
    return lax.ppermute(array, "grp", [(g, g ^ flip) for g in range(GROUPS)])


def send_wide(array, way):
    if way == "gather":
        return [array, lax.all_gather(array, "grp", axis=0, tiled=True)]
    return [array, permute(array, 1), permute(array, 2)]


def spread_wide(array, *others):
    count, rows, _ = array.shape
    if len(others) == 1:
        return [(array, slots(rows))] + [
            (others[0], group_slots(rows, flip, count)) for flip in (1, 2, 3)
        ]
    near, across = others
    return [(a, slots(rows)) for a in (array, near, across, permute(across, 1))]


def gather_small(array):
    near = permute(array, 1)
    return [(a, slots(array.shape[1])) for a in (array, near, permute(array + near, 2))]


def scatter_over_seq(packed):
    ranks = lax.axis_size("seq")
    rows, columns = packed.shape
    return lax.all_to_all(packed.reshape(ranks, rows // ranks, columns), "seq", 0, 0)


def sum_over_seq(chain, scalars, shares, held=()):
    ranks, rows, columns = shares.shape
    block = whole(ranks, rows, columns)
    place = pl.BlockSpec(memory_space=pl.ANY)
    *passed, own = call(
        chain, share_kernel, "share", 1, scalars, [(shares, block)] + [(h, place) for h in held],
        [(h.shape, h.dtype, place) for h in held] + [(shares.shape, BF16, block)],
        aliases={len(scalars) + 1 + n: n for n in range(len(held))}, us=1.0,
    )
    return lax.all_to_all(own, "seq", 0, 0).reshape(ranks * rows, columns), passed


def hold(chain, scalars, arrays):
    place = pl.BlockSpec(memory_space=pl.ANY)
    return call(
        chain, hold_kernel, "hold", 1, scalars, [(a, place) for a in arrays],
        [(a.shape, a.dtype, place) for a in arrays],
        aliases={len(scalars) + n: n for n in range(len(arrays))},
    )


def local(
    tokens, lengths, w_qkv, b_qv, w_out, b_out, ln1_gain, ln1_bias, w_up, b_up, w_down, b_down,
    ln2_gain, ln2_bias, cotangent,
):
    width, row_count = tokens.shape
    units = w_up.shape[1]
    seq_count = lengths.shape[0]
    group = lax.axis_index("grp").astype(jnp.int32)
    scalars = (lengths, group[None])
    parts = units // width
    rows = jnp.concatenate(
        [b_qv.reshape(-1), b_out, ln1_gain, ln1_bias, b_down, ln2_gain, ln2_bias, b_up]
    ).reshape(8 + parts, width)
    chain = []
    middle = int(seq_count * FIRST_CHUNK)
    chunks = [(0, middle), (middle, seq_count - middle)]
    untouched = pl.BlockSpec(memory_space=pl.ANY)
    state = [{}, {}]
    shared = dict(output=None, grad_tokens=None, packed=None, packed_qkv=None)
    pack_width = 2 * units + GROUPS * width + LANE
    qkv_width = 3 * width + LANE // 2
    square = ((width, width), BF16, whole(width, width))

    def prepare(_):
        turned = ((units, width), BF16, whole(units, width))
        shared["vec"], shared["bup"], shared["wo"], wo_t, shared["wup_t"], shared["wdown_t"] = call(
            chain, prepare_kernel, "prepare", 1, scalars,
            [
                (rows, whole(8 + parts, width)), (w_out, whole(width, D)),
                (w_up, whole(width, units)), (w_down, whole(width, units)),
            ],
            [
                ((width, 8 + parts), F32, whole(width, 8 + parts)),
                ((units, 1), F32, whole(units, 1)),
                ((GROUPS, width, width), BF16, whole(GROUPS, width, width)),
                ((2, width, width), BF16, whole(2, width, width)), turned, turned,
            ],
            scratch=[pltpu.VMEM((D, width), BF16)], vmem=VMEM,
        )
        shared["mixers"] = [
            (wo_t, pl.BlockSpec((None, width, width), lambda i, lens, group: (0, 0, 0))),
            (permute(wo_t[1], 1), whole(width, width)),
        ]

    def attend(which):
        first, count = chunks[which]
        steps = count + 1 if which == 0 else count
        near_end = lambda i, lens, group: (0, first + jnp.minimum(i, count - 1))
        held = lambda height: pl.BlockSpec(
            (None, height, SLOT), lambda i, lens, group: (jnp.minimum(i, count - 1), 0, 0)
        )
        context, lse = call(
            chain, functools.partial(attend_forward_kernel, first, count), "attend_forward", steps,
            scalars,
            [
                (tokens, pl.BlockSpec((width, SLOT), near_end)), (w_qkv, whole(width, 3 * width)),
                (b_qv, whole(2, width)), (w_out, whole(width, D)),
            ],
            [
                ((steps, width, SLOT), BF16, slots(width)),
                ((count, 8, SLOT), F32, held(8)),
            ],
            scratch=[
                pltpu.VMEM((3 * width, width), BF16), pltpu.VMEM((width, 8), F32),
                pltpu.VMEM((D, width), BF16),
            ],
            us=ATTEND_US, vmem=ATTEND_VMEM[which],
        )
        state[which].update(context=send_wide(context, CONTEXT_WAYS[which]), lse=lse)

    def hold_context(which):
        mine = state[which]
        if CONTEXT_WAYS[which] == "permute" and which in CONTEXT_HELD:
            mine["context"][2:] = hold(chain, scalars, mine["context"][2:])
        mine["contexts"] = spread_wide(*mine["context"])
        if which == 0:
            place = chunks[0][1]
            shared["mixers"] += [
                (array, slot_at(place, width)) for array, _ in mine["contexts"][2:]
            ]

    def mix(which):
        (first, count), mine = chunks[which], state[which]
        mine["resid"], stats = call(
            chain, functools.partial(mix_kernel, first), "mix", count, scalars,
            mine["contexts"] + [(tokens, columns_of(width, first))] + shared["mixers"]
            + [(shared["vec"], whole(width, 8 + parts))],
            [((count, width, SLOT), F32, slots(width)), ((count, 2, SLOT), F32, slots(2))],
            us=3.0 * MIDDLE_US,
        )
        mine["one"] = gather_small(stats)

    def feed_forward(which):
        (first, count), mine = chunks[which], state[which]
        mine["hid"], mine["two"], stats = call(
            chain, functools.partial(feed_forward_kernel, first), "feed_forward", count, scalars,
            [(mine["resid"], slots(width))] + mine["one"] + [
                (cotangent, columns_of(width, first)), (shared["wup_t"], whole(units, width)),
                (w_down, whole(width, units)), (shared["vec"], whole(width, 8 + parts)),
                (shared["bup"], whole(units, 1)),
            ],
            [
                ((count, width, SLOT), BF16, slots(width)),
                ((count, width, SLOT), F32, slots(width)),
                ((count, 4, SLOT), F32, slots(4)),
            ],
            us=8.0 * MIDDLE_US,
        )
        mine["second"] = gather_small(stats)

    def feed_backward(which):
        (first, count), mine = chunks[which], state[which]
        grads = ((width, 2 * units + LANE), F32, whole(width, 2 * units + LANE))
        ins = [(mine["two"], slots(width))] + mine["second"] + [
            (cotangent, columns_of(width, first)), (mine["hid"], slots(width)),
            (mine["resid"], slots(width)),
        ] + mine["one"] + [
            (shared["wup_t"], whole(units, width)), (shared["wdown_t"], whole(units, width)),
            (w_up, whole(width, units)), (shared["vec"], whole(width, 8 + parts)),
            (shared["bup"], whole(units, 1)),
        ]
        aliases, has_earlier = {}, shared["output"] is not None
        if has_earlier:
            ins.append((shared["grads"], grads[2]))
            aliases = {len(scalars) + len(ins): 0}
            ins.append((shared["output"], untouched))
        shared["output"], mine["ghid"], stats, shared["grads"] = call(
            chain, functools.partial(feed_backward_kernel, first, has_earlier), "feed_backward",
            count, scalars, ins,
            [
                ((width, row_count), BF16, columns_of(width, first)),
                ((count, width, SLOT), BF16, slots(width)),
                ((count, 2, SLOT), F32, slots(2)), grads,
            ],
            scratch=[pltpu.VMEM((5, width, LANE), F32), pltpu.VMEM((units, LANE), F32)],
            aliases=aliases, us=8.0 * MIDDLE_US,
        )
        mine["third"] = gather_small(stats)

    def wait_third(_):
        chain.extend(state[which]["third"][2][0] for which in (0, 1))

    def residual_grad(which):
        (first, count), mine = chunks[which], state[which]
        gone, mine["out"] = call(
            chain, functools.partial(residual_grad_kernel, first), "residual_grad", count, scalars,
            [(mine["ghid"], slots(width))] + mine["third"] + [(mine["resid"], slots(width))]
            + mine["one"] + [(shared["vec"], whole(width, 8 + parts))],
            [((count, width, SLOT), BF16, slots(width)), ((width, LANE), F32, whole(width, LANE))],
            us=2.0 * MIDDLE_US,
        )
        mine["gone"] = send_wide(gone, GRADIENT_WAYS[which])

    def weight_grad(which):
        (first, count), mine = chunks[which], state[which]
        final = shared["packed"] is not None
        ins = [
            (mine["gone"][0], slots(width)), *mine["contexts"], (mine["out"], whole(width, LANE)),
        ]
        result = ((GROUPS, width, width), F32, whole(GROUPS, width, width))
        if final:
            ins += [
                (shared["packed"], result[2]),
                (shared["grads"], whole(width, 2 * units + LANE)),
                (state[1 - which]["out"], whole(width, LANE)),
            ]
            result = ((width, pack_width), BF16, whole(width, pack_width))
        (shared["packed"],) = call(
            chain, functools.partial(weight_grad_kernel, first), "weight_grad", count, scalars, ins,
            [result], scratch=[pltpu.VMEM((GROUPS, width, width), F32)], us=WEIGHT_US[final],
        )
        if final:
            shared["shares"] = scatter_over_seq(shared["packed"])

    def share(which):
        mine = state[which]
        shared["weight_sums"], far = sum_over_seq(
            chain, scalars, shared["shares"], mine["gone"][2:] if which in GRADIENT_HELD else ()
        )
        if far:
            mine["gone"][2:] = far

    def hold_gone(which):
        mine = state[which]
        mine["gone"][2:] = hold(chain, scalars, mine["gone"][2:])

    def attend_backward(which):
        (first, count), mine = chunks[which], state[which]
        final = shared["packed_qkv"] is not None
        ins = [
            *spread_wide(*mine["gone"]), (mine["contexts"][0][0], slots(width)),
            (mine["lse"], slots(8)),
            (tokens, columns_of(width, first)), (shared["wo"], whole(GROUPS, width, width)),
            (w_qkv, whole(width, 3 * width)), (b_qv, whole(2, width)),
        ]
        aliases = {}
        if final:
            ins.append((shared["packed_qkv"], whole(width, qkv_width)))
            aliases = {len(scalars) + len(ins): 0}
            ins.append((shared["grad_tokens"], untouched))
        shared["grad_tokens"], shared["packed_qkv"] = call(
            chain, functools.partial(attend_backward_kernel, first, final), "attend_backward", count,
            scalars, ins,
            [
                ((width, row_count), BF16, columns_of(width, first)),
                ((width, qkv_width), BF16 if final else F32, whole(width, qkv_width)),
            ],
            scratch=[
                pltpu.VMEM((width, 3 * width), F32), pltpu.VMEM((2, width, LANE), F32),
                pltpu.VMEM((3 * width, SLOT), BF16),
                pltpu.VMEM((3 * width, width), BF16), pltpu.VMEM((width, 8), F32),
            ],
            aliases=aliases, us=BACKWARD_US[final], vmem=BACKWARD_VMEM[final],
        )

    stages = dict(
        P=prepare, A=attend, H=hold_context, M=mix, U=feed_forward, B=feed_backward, R=residual_grad,
        T=wait_third, W=weight_grad, S=share, G=hold_gone, D=attend_backward,
    )
    for stage in ORDER:
        stages[stage[0]](int(stage[1]))
    output, grad_tokens = shared["output"], shared["grad_tokens"]
    shares_qkv = scatter_over_seq(shared["packed_qkv"])
    *blocks, small, grad_w_up, grad_w_down = call(
        chain, unpack_kernel, "unpack", 1, scalars,
        [(shared["weight_sums"], whole(width, pack_width))],
        [
            square, square, square, square,
            ((LANE, width), F32, whole(LANE, width)),
            ((width, units), F32, whole(width, units)),
            ((width, units), F32, whole(width, units)),
        ],
        us=3.0,
    )
    routed = [blocks[0]] + [permute(blocks[flip], flip) for flip in (1, 2, 3)]
    chain += routed[1:]
    qkv_sums, _ = sum_over_seq(chain, scalars, shares_qkv)
    (grad_w_out,) = call(
        chain, assemble_kernel, "assemble", 1, scalars,
        [(block, whole(width, width)) for block in routed],
        [((width, D), F32, whole(width, D))],
        scratch=[pltpu.VMEM((GROUPS, width, width), F32)], us=1.0,
    )
    grad_b_qv, grad_w_qkv = call(
        chain, unpack_qkv_kernel, "unpack_qkv", 1, scalars, [(qkv_sums, whole(width, qkv_width))],
        [((2, width), F32, whole(2, width)), ((width, 3 * width), F32, whole(width, 3 * width))],
    )
    return (
        output, grad_tokens, grad_w_qkv, grad_b_qv, grad_w_out, small[5], small[3], small[4],
        grad_w_up, small[6 : 6 + parts].reshape(-1), grad_w_down, small[2], small[0], small[1],
    )


def solution(mesh):
    row, vector = P("grp", None), P("grp")
    placed = (
        P("grp", "seq"), P("seq"), row, P(None, "grp"), row, vector, vector, vector, row, vector,
        row, vector, vector, vector, P("grp", "seq"),
    )
    results = (
        P("grp", "seq"), P("grp", "seq"), row, P(None, "grp"), row, vector, vector, vector, row,
        vector, row, vector, vector, vector,
    )
    return jax.shard_map(local, mesh=mesh, in_specs=placed, out_specs=results, check_vma=False)
```
